32 devices in a mesh: group: 4 (over z), width: 8 (over y, x, core).
Axes of the slice: x: 2, y: 2, z: 4, core: 2. Of those that a mesh axis runs over, the one named last changes fastest.
Arguments:
- momentum: bfloat16 [12, 1024, 7168], P('group', None, 'width'), may hold values from -0.049560547 to 0.049560547
- assignment: int32 [12], replicated, may hold values from -1 to 3, as said below
Outputs:
- update: bfloat16 [12, 1024, 7168], P('group', None, 'width')
- slot_update: bfloat16 [4, 2, 1024, 7168], P('group', None, None, 'width')
The draws below stay inside these ranges and needn't reach their ends.
Inputs may be any that keep to these rules, and one draw needn't show every extreme that they name: `assignment`: owner o holds slots o * 3 to o * 3 + 2 and uses its first 1 to 3 of them (the others are -1), some owner all 3; 6 slots are used in all; no group is named by more than 2 slots, and some group by exactly 2.
All inputs are finite; a program needn't handle non-finite values.
Results may differ from the reference program's by a relative error of at most 0.0058.
Values may be sent and summed in bfloat16 or wider, within the bound.
No kernel may reach another device: no remote copies, remote signals or barrier semaphores. Data moves between devices by JAX's collectives and lax.ppermute only.
A program may use at most 128 MiB of HBM per device.

```python
import math
import jax
import jax.numpy as jnp
from jax import lax

D = 7168
H = 1024
HOLD = 3
CAP = 2
EXPERTS = 12
LIVE = 6
N_GROUP = 4


def assignment_table(key):
    key_gpick, key_gperm, key_opick, key_operm, key_list = jax.random.split(key, 5)
    quads = N_GROUP // 4
    first_quad = jnp.arange(quads, dtype=jnp.int32) == 0
    group_patterns = jnp.array([[2, 2, 1, 1], [2, 2, 2, 0]], dtype=jnp.int32)
    gpick = jax.random.randint(key_gpick, (quads,), 0, 2)
    gpick = jnp.where(first_quad, 0, gpick)
    gcounts = group_patterns[gpick].reshape(N_GROUP)
    gcounts = gcounts[jax.random.permutation(key_gperm, N_GROUP)]
    owner_patterns = jnp.array([[3, 1, 1, 1], [2, 2, 1, 1]], dtype=jnp.int32)
    opick = jax.random.randint(key_opick, (quads,), 0, 2)
    opick = jnp.where(first_quad, 0, opick)
    ocounts = owner_patterns[opick].reshape(N_GROUP)
    ocounts = ocounts[jax.random.permutation(key_operm, N_GROUP)]
    positions = jnp.arange(EXPERTS, dtype=jnp.int32)
    live = positions % HOLD < ocounts[positions // HOLD]
    rank = jnp.cumsum(live.astype(jnp.int32)) - 1
    rank = jnp.clip(rank, 0, LIVE - 1).astype(jnp.int32)
    ends = jnp.cumsum(gcounts)
    entries = jnp.arange(LIVE, dtype=jnp.int32)
    listed = jnp.sum((ends[None, :] <= entries[:, None]).astype(jnp.int32), axis=1).astype(jnp.int32)
    listed = listed[jax.random.permutation(key_list, LIVE)]
    target = listed[0]
    partner = (target + N_GROUP // 2) % N_GROUP
    where_to = rank[partner * HOLD]
    other = listed[where_to]
    swapped = jnp.where(entries == where_to, target, listed)
    swapped = jnp.where(entries == 0, other, swapped)
    return jnp.where(live, swapped[rank], -1).astype(jnp.int32)


def draw_assignment(key, part):
    return assignment_table(key)


def block_scale(stream_key, extent, cuts, smallest, high):
    level = 1.0
    for position, blocks in cuts:
        draws = jax.random.uniform(jax.random.fold_in(jax.random.fold_in(stream_key, 6), position), (blocks,), jnp.float32, smallest / len(cuts), high / len(cuts))
        level = level * jnp.repeat(jnp.exp(draws), extent[position] // blocks).reshape((-1,) + (1,) * (len(extent) - 1 - position))
    return level


def normal_values(rng, extent, width, reach, pieces=(), kind=jnp.bfloat16):
    result = width * jax.random.normal(rng, extent, jnp.float32)
    if pieces:
        result = result * block_scale(rng, extent, pieces, -0.22, 0.18)
    return jnp.clip(result, -reach, reach).astype(kind)


def setup_inputs(seed: int = 0) -> dict:
    keys = jax.random.split(jax.random.key(seed), 3)
    momentum = normal_values(keys[0], (EXPERTS, H, D), (0.7 / D ** 0.5), 0.049560547, ((0, 4), (2, 8)))
    assignment = draw_assignment(jax.random.fold_in(keys[2], 71), 0)
    return dict(momentum=momentum, assignment=assignment)


def slots_of(assignment):
    count = assignment.shape[0]
    order = jnp.arange(count, dtype=jnp.int32)
    earlier = order[:, None] > order[None, :]
    same = assignment[:, None] == assignment[None, :]
    return lax.optimization_barrier(jnp.sum((earlier & same).astype(jnp.int32), axis=1)).astype(jnp.int32)

def newton_step(block):
    gram = jnp.dot(block, block.T, preferred_element_type=jnp.float32)
    gram_b = gram.astype(jnp.bfloat16)
    first = jnp.dot(gram_b, block, preferred_element_type=jnp.float32).astype(jnp.bfloat16)
    second = jnp.dot(gram_b, first, preferred_element_type=jnp.float32)
    mixed = 3.4445 * block.astype(jnp.float32) - 4.775 * first.astype(jnp.float32) + 2.0315 * second
    return (math.sqrt(D) * mixed).astype(jnp.bfloat16)

def reference(momentum, assignment):
    live = (assignment >= 0).astype(jnp.float32)
    update = lax.map(newton_step, momentum)
    update = (update.astype(jnp.float32) * live[:, None, None]).astype(jnp.bfloat16)
    slot = slots_of(assignment)
    groups = jnp.arange(N_GROUP, dtype=jnp.int32)
    places = jnp.arange(CAP, dtype=jnp.int32)
    chosen = (assignment[None, None, :] == groups[:, None, None]) & (slot[None, None, :] == places[None, :, None])
    table = chosen.astype(jnp.bfloat16).reshape(N_GROUP * CAP, EXPERTS)
    flat = jnp.dot(table, update.reshape(EXPERTS, H * D), preferred_element_type=jnp.float32)
    slot_update = flat.astype(jnp.bfloat16).reshape(N_GROUP, CAP, H, D)
    return (update, slot_update)
```

```python
import functools
import math

import jax
import jax.numpy as jnp
from jax import lax
from jax.experimental import pallas as pl
from jax.experimental.pallas import tpu as pltpu
from jax.sharding import PartitionSpec as P

D = 7168
CAP = 2
CHUNKS = 2
DELAY = 2
STEPS = 4
EXTRA = (0, 2, 4, 6)
BLOCK = 256
SCALE = math.sqrt(D)
VMEM_BYTES = 56 * 1024 * 1024
NEVER = 1 << 20
FAR = 1 << 10
WORK = 5 * 10**9

SMEM = pl.BlockSpec(memory_space=pltpu.SMEM)
VMEM = pl.BlockSpec(memory_space=pltpu.VMEM)
ANY = pl.BlockSpec(memory_space=pl.ANY)


def compiler_params():
    return pltpu.CompilerParams(vmem_limit_bytes=VMEM_BYTES)


def most_steps(n, hold):
    end = 0
    for link in range(n - 1):
        load = min(hold * (link + 1), CAP * (n - 1 - link))
        end = max(CHUNKS, end - CHUNKS + DELAY) + CHUNKS * load
    return max(end, STEPS + max(EXTRA))


def plan_kernel(n, hold, assign, where, snd, meta, slot, key, ready, start, front):
    experts = n * hold
    me = where[0]
    names = [assign[e] for e in range(experts)]
    for e in range(experts):
        count = jnp.int32(0)
        for e2 in range(e):
            count += (names[e2] == names[e]).astype(jnp.int32)
        slot[e] = count
    for s in range(CAP):
        meta[2 + s] = -1
    for e in range(experts):

        @pl.when((names[e] == me) & (e // hold == me) & (slot[e] < CAP))
        def _():
            meta[2 + slot[e]] = e % hold

    for h in range(hold):
        meta[2 + CAP + h] = (assign[me * hold + h] >= 0).astype(jnp.int32)

    def crossing(e, side, link):
        owner = e // hold
        frm = owner if side == 0 else n - 1 - owner
        if frm > link:
            return None
        to = names[e] if side == 0 else n - 1 - names[e]
        return (names[e] >= 0) & (link < to)

    busy = []
    for side in range(2):
        most = jnp.int32(0)
        for link in range(n - 1):
            load = jnp.int32(0)
            for e in range(experts):
                here = crossing(e, side, link)
                if here is not None:
                    load += here.astype(jnp.int32)
            most = jnp.maximum(most, load)
        busy.append(most)

    for owner in range(n):
        best, chosen = jnp.int32(-2), jnp.int32(0)
        for h in range(hold):
            name = names[owner * hold + h]
            value = jnp.where(
                name > owner, busy[0] * 64 + name - owner, jnp.where(name < owner, busy[1] * 64 + owner - name, 0)
            )
            value = jnp.where(name < 0, -1, value)
            best, chosen = jnp.where(value > best, value, best), jnp.where(value > best, h, chosen)
        front[owner] = chosen
    chosen = front[me]
    meta[2 + CAP + hold] = chosen
    for place in range(1, hold):
        meta[2 + CAP + hold + place] = jnp.where(chosen >= place, place - 1, place)

    longest = jnp.int32(0)
    for side in range(2):
        mine = me if side == 0 else n - 1 - me

        def clear(t, _):
            snd[side, t] = 0
            return 0

        lax.fori_loop(0, snd.shape[1], clear, 0)
        for link in range(n - 1):
            for e in range(experts):
                here = crossing(e, side, link)
                if here is None:
                    key[e] = NEVER
                    continue
                owner = e // hold
                frm = owner if side == 0 else n - 1 - owner
                to = names[e] if side == 0 else n - 1 - names[e]
                if frm == link:
                    at = jnp.where(front[owner] == e % hold, 0, CHUNKS)
                else:
                    at = start[e] + DELAY
                ready[e] = at
                key[e] = jnp.where(here, at * 64 + (n - to), NEVER)

            def choose(_, cursor):
                low, e = key[0], jnp.int32(0)
                for e2 in range(1, experts):
                    better = key[e2] < low
                    low, e = jnp.where(better, key[e2], low), jnp.where(better, e2, e)
                begin = jnp.maximum(cursor, ready[e])

                @pl.when(low < NEVER)
                def _():
                    before = start[e]
                    key[e] = NEVER
                    start[e] = begin
                    local = e // hold == me
                    to = assign[e] if side == 0 else n - 1 - assign[e]

                    @pl.when(mine == link)
                    def _():
                        base = jnp.where(local, e % hold * CHUNKS, NEVER + before)
                        for j in range(CHUNKS):
                            snd[side, begin + j] = base + j

                    @pl.when((mine == link + 1) & (to == link + 1) & (slot[e] < CAP))
                    def _():
                        meta[2 + slot[e]] = hold + FAR * side + begin

                return jnp.where(low < NEVER, begin + CHUNKS, cursor)

            most = min(hold * (link + 1), CAP * (n - 1 - link))
            longest = jnp.maximum(longest, lax.fori_loop(0, most, choose, jnp.int32(0)))
    branch = jnp.int32(0)
    for extra in EXTRA:
        branch += (longest > STEPS + extra).astype(jnp.int32)
    meta[0] = branch
    meta[1] = where[1]
    meta[2 + CAP + 2 * hold] = longest


def make_plan(assignment, where, n, hold):
    i32 = jnp.int32
    return pl.pallas_call(
        functools.partial(plan_kernel, n, hold),
        out_shape=[
            jax.ShapeDtypeStruct((2, most_steps(n, hold)), i32),
            jax.ShapeDtypeStruct((3 + CAP + 2 * hold,), i32),
        ],
        in_specs=[SMEM, SMEM],
        out_specs=[SMEM] * 2,
        scratch_shapes=[pltpu.SMEM((n * hold,), i32) for _ in range(4)] + [pltpu.SMEM((n,), i32)],
        name="plan",
    )(assignment, where)


def pick_kernel(step, count, snd, own, *rest):
    came, (right, left, sems) = rest[: 2 * count], rest[-3:]
    for side, target in enumerate((right, left)):
        code = snd[side, step]

        @pl.when(code < NEVER)
        def _():
            pltpu.make_async_copy(own.at[code], target, sems.at[side]).start()

        for t in range(count):

            @pl.when(code == NEVER + t)
            def _():
                pltpu.make_async_copy(came[2 * t + side], target, sems.at[side]).start()

    for side, target in enumerate((right, left)):
        pltpu.make_async_copy(own.at[0], target, sems.at[side]).wait()


def pick(own, snd, came, step):
    count = max(step + 1 - DELAY, 0)
    earlier = [x for pair in came[:count] for x in pair]
    chunk = jax.ShapeDtypeStruct(own.shape[1:], own.dtype)
    return pl.pallas_call(
        functools.partial(pick_kernel, step, count),
        out_shape=[chunk, chunk],
        in_specs=[SMEM] + [ANY] * (1 + len(earlier)),
        out_specs=[VMEM, VMEM],
        scratch_shapes=[pltpu.SemaphoreType.DMA((2,))],
        cost_estimate=pl.CostEstimate(
            flops=0, bytes_accessed=1, transcendentals=0
        ),
        name="pick",
    )(snd, own, *earlier)


def hop(right, left, n):
    return (
        lax.ppermute(right, "group", [(i, i + 1) for i in range(n - 1)]),
        lax.ppermute(left, "group", [(i + 1, i) for i in range(n - 1)]),
    )


def place_kernel(hold, steps, meta, update_ref, *rest):
    came, (out_ref, sems) = rest[: 2 * steps], rest[2 * steps :]
    chunk = out_ref.shape[1] // CHUNKS

    def target(s, j):
        return out_ref.at[s, pl.ds(j * chunk, chunk)]

    for s in range(CAP):
        kind = meta[2 + s]

        @pl.when((kind >= 0) & (kind < hold))
        def _():
            for j in range(CHUNKS):
                pltpu.make_async_copy(
                    update_ref.at[kind, pl.ds(j * chunk, chunk)], target(s, j), sems.at[s, j]
                ).start()

        for side in range(2):
            for j in range(CHUNKS):
                for t in range(j, steps):

                    @pl.when(kind == hold + FAR * side + t - j)
                    def _():
                        pltpu.make_async_copy(came[2 * t + side], target(s, j), sems.at[s, j]).start()

        @pl.when(kind < 0)
        def _():
            out_ref[s] = jnp.zeros(out_ref.shape[1:], out_ref.dtype)

    for s in range(CAP):
        kind = meta[2 + s]
        at = kind - hold
        at = jnp.where(at >= FAR, at - FAR, at)
        for j in range(CHUNKS):

            @pl.when((kind >= 0) & (at + j < steps))
            def _():
                pltpu.make_async_copy(came[0], target(s, j), sems.at[s, j]).wait()


def last_kernel(hold, last, meta, _, *rest):
    came, (out_ref, sems) = rest[:2], rest[2:]
    chunk = came[0].shape[0]
    for wait in (False, True):
        for s in range(CAP):
            for side in range(2):
                for j in range(CHUNKS):

                    @pl.when((meta[2 + s] >= hold) & (meta[2 + s] == hold + FAR * side + last - j))
                    def _():
                        copy = pltpu.make_async_copy(
                            came[side], out_ref.at[s, pl.ds(j * chunk, chunk)], sems.at[s]
                        )
                        copy.wait() if wait else copy.start()


def place(meta, came, update):
    hold, rows, cols = update.shape
    arrived = [x for pair in came for x in pair]
    return pl.pallas_call(
        functools.partial(place_kernel, hold, len(came)),
        out_shape=jax.ShapeDtypeStruct((CAP, rows, cols), update.dtype),
        in_specs=[SMEM, ANY] + [ANY] * len(arrived),
        out_specs=VMEM,
        scratch_shapes=[pltpu.SemaphoreType.DMA((CAP, CHUNKS))],
        compiler_params=compiler_params(),
        cost_estimate=pl.CostEstimate(flops=WORK, bytes_accessed=1, transcendentals=0),
        name="place",
    )(meta, update, *arrived)


def place_last(meta, out, came, step, hold):
    return pl.pallas_call(
        functools.partial(last_kernel, hold, step),
        out_shape=jax.ShapeDtypeStruct(out.shape, out.dtype),
        in_specs=[SMEM, ANY, VMEM, VMEM],
        out_specs=ANY,
        scratch_shapes=[pltpu.SemaphoreType.DMA((CAP,))],
        input_output_aliases={1: 0},
        cost_estimate=pl.CostEstimate(flops=WORK, bytes_accessed=1, transcendentals=0),
        name="last",
    )(meta, out, *came)


def pieces_of(me, q, width):
    chips = width // 2
    core, chip = q // chips, q % chips
    return ((me & 1) ^ core) * chips + ((me >> 1) ^ chip)


def gram_kernel(blocks, width, meta, x_ref, *rest):
    outs, scratch = rest[:4], rest[4]
    high = BLOCK // width
    me = meta[1]
    for j in range(blocks):
        rows = (j + 1) * BLOCK
        scratch[j, pl.ds(0, rows), :] = lax.dot_general(
            x_ref[0, pl.ds(0, rows), :],
            x_ref[0, pl.ds(j * BLOCK, BLOCK), :],
            (((1,), (1,)), ((), ())),
            preferred_element_type=jnp.float32,
        ).astype(jnp.bfloat16)

    def sort(keep, send):
        for j in range(blocks):
            for q in range(width):
                piece = pieces_of(me, q, width)
                out = keep if q < width // 2 else send
                base = q % (width // 2) * (blocks * (blocks + 1) // 2)
                for i in range(j + 1):
                    at = base + j * (j + 1) // 2 + i
                    out[0, pl.ds(at * high, high), :] = scratch[
                        j, pl.ds(pl.multiple_of(i * BLOCK + piece * high, high), high), :
                    ]

    pl.when(pl.program_id(0) == 0)(lambda: sort(*outs[:2]))
    pl.when(pl.program_id(0) > 0)(lambda: sort(*outs[2:]))


def partial_gram(meta, momentum, width):
    hold, rows, cols = momentum.shape
    blocks = rows // BLOCK
    packed = blocks * (blocks + 1) // 2 * BLOCK
    shapes = [jax.ShapeDtypeStruct((count, packed // 2, BLOCK), jnp.bfloat16) for count in (1, 1, hold - 1, hold - 1)]
    one = pl.BlockSpec((1, packed // 2, BLOCK), lambda e, meta: (0, 0, 0))
    others = pl.BlockSpec((1, packed // 2, BLOCK), lambda e, meta: (jnp.maximum(e - 1, 0), 0, 0))
    return pl.pallas_call(
        functools.partial(gram_kernel, blocks, width),
        grid_spec=pltpu.PrefetchScalarGridSpec(
            num_scalar_prefetch=1,
            grid=(hold,),
            in_specs=[pl.BlockSpec((1, rows, cols), lambda e, meta: (meta[2 + CAP + hold + e], 0, 0))],
            out_specs=[one, one, others, others],
            scratch_shapes=[pltpu.VMEM((blocks, rows, BLOCK), jnp.bfloat16)],
        ),
        out_shape=shapes,
        compiler_params=compiler_params(),
        cost_estimate=pl.CostEstimate(
            flops=2 * hold * packed * BLOCK * cols,
            bytes_accessed=2 * hold * (rows * cols + packed * BLOCK),
            transcendentals=0,
        ),
        name="gram",
    )(meta, momentum)


def exchange(x, other, width):
    return lax.ppermute(x, "width", [(i, i ^ other) for i in range(width)])


def reduce_scatter(keep, send, width):
    chips = width // 2
    high = keep.shape[1] // chips
    total = keep.astype(jnp.float32) + exchange(send, 1, width).astype(jnp.float32)
    mine = total[:, :high]
    for r in range(1, chips):
        piece = total[:, r * high : (r + 1) * high].astype(jnp.bfloat16)
        mine = mine + exchange(piece, 2 * r, width).astype(jnp.float32)
    return mine.astype(jnp.bfloat16)


def all_gather(x, width):
    pieces = [x] + [exchange(x, 2 * r, width) for r in range(1, width // 2)]
    return pieces + [exchange(piece, 1, width) for piece in pieces]


def unpack(blocks, width, me, pieces, gram_ref):
    high = BLOCK // width
    for q in range(width):
        piece = pieces_of(me, q, width)
        for j in range(blocks):
            for i in range(j + 1):
                at = j * (j + 1) // 2 + i
                gram_ref[
                    pl.ds(pl.multiple_of(i * BLOCK + piece * high, high), high), pl.ds(j * BLOCK, BLOCK)
                ] = pieces[q][0, pl.ds(at * high, high), :]
    for j in range(blocks):
        for i in range(j):
            gram_ref[pl.ds(j * BLOCK, BLOCK), pl.ds(i * BLOCK, BLOCK)] = gram_ref[
                pl.ds(i * BLOCK, BLOCK), pl.ds(j * BLOCK, BLOCK)
            ].T


def update_kernel(blocks, width, hold, place, meta, x_ref, *rest):
    pieces, (gram_ref, first_ref, second_ref, sems) = rest[:width], rest[-4:]
    outs = rest[width + (place > 0) : -4]
    chosen = meta[2 + CAP + hold + place]
    live = meta[2 + CAP + chosen]
    rows = x_ref.shape[1]
    chunk = rows // CHUNKS

    def copies(j):
        span = pl.ds(j * chunk, chunk)
        targets = [outs[0].at[chosen, span]]
        if place == 0:
            targets.append(outs[1 + j])
        return [pltpu.make_async_copy(second_ref.at[span], to, sems.at[j, i]) for i, to in enumerate(targets)]

    @pl.when(live == 1)
    def _():
        unpack(blocks, width, meta[1], pieces, gram_ref)
        first_ref[...] = jnp.dot(gram_ref[...], x_ref[0], preferred_element_type=jnp.float32).astype(jnp.bfloat16)

    for j in range(CHUNKS):
        span = pl.ds(j * chunk, chunk)

        @pl.when(live == 1)
        def _():
            second = jnp.dot(gram_ref[span, :], first_ref[...], preferred_element_type=jnp.float32)
            x, first = x_ref[0, span, :].astype(jnp.float32), first_ref[span, :].astype(jnp.float32)
            mixed = 3.4445 * x - 4.775 * first + 2.0315 * second
            second_ref[span, :] = (SCALE * mixed).astype(jnp.bfloat16)

        @pl.when(live == 0)
        def _():
            second_ref[span, :] = jnp.zeros((chunk, second_ref.shape[1]), jnp.bfloat16)

        for copy in copies(j):
            copy.start()
    for j in range(CHUNKS):
        for copy in copies(j):
            copy.wait()


def one_update(meta, pieces, momentum, place, update=None):
    hold, rows, cols = momentum.shape
    index = max(place - 1, 0)
    width = len(pieces)
    out_shape = [jax.ShapeDtypeStruct(momentum.shape, momentum.dtype)]
    if place == 0:
        out_shape += [jax.ShapeDtypeStruct((rows // CHUNKS, cols), momentum.dtype)] * CHUNKS
    before = [] if update is None else [update]
    return pl.pallas_call(
        functools.partial(update_kernel, rows // BLOCK, width, hold, place),
        grid_spec=pltpu.PrefetchScalarGridSpec(
            num_scalar_prefetch=1,
            grid=(1,),
            in_specs=[pl.BlockSpec((1, rows, cols), lambda i, meta: (meta[2 + CAP + hold + place], 0, 0))]
            + [pl.BlockSpec((1,) + piece.shape[1:], lambda i, meta: (index, 0, 0)) for piece in pieces]
            + [ANY] * len(before),
            out_specs=[ANY] * len(out_shape),
            scratch_shapes=[
                pltpu.VMEM((rows, rows), jnp.bfloat16),
                pltpu.VMEM((rows, cols), jnp.bfloat16),
                pltpu.VMEM((rows, cols), jnp.bfloat16),
                pltpu.SemaphoreType.DMA((CHUNKS, 2)),
            ],
        ),
        out_shape=out_shape,
        input_output_aliases={2 + width: 0} if before else {},
        compiler_params=compiler_params(),
        cost_estimate=pl.CostEstimate(
            flops=4 * rows * rows * cols, bytes_accessed=6 * rows * cols, transcendentals=0
        ),
        name="update",
    )(meta, momentum, *pieces, *before)


def stream(meta, snd, update, came, out, extra, n):
    hold, rows, cols = update.shape
    chunks = update.reshape(-1, rows // CHUNKS, cols)
    came = list(came)
    for step in range(STEPS, STEPS + extra):
        came.append(hop(*pick(chunks, snd, came, step), n))
    for step in range(STEPS, STEPS + extra):
        out = place_last(meta, out, came[step], step, hold)
    return out[None]


def endless_pick_kernel(count, snd, step, own, came_in, *rest):
    came, (right, left, sems) = rest[:-3], rest[-3:]
    for side, target in enumerate((right, left)):
        code = snd[side, step[0]]

        @pl.when(code < NEVER)
        def _():
            pltpu.make_async_copy(own.at[code], target, sems.at[side]).start()

        @pl.when(code >= NEVER + count)
        def _():
            pltpu.make_async_copy(came_in.at[side, code - NEVER - count], target, sems.at[side]).start()

        for t in range(count):

            @pl.when(code == NEVER + t)
            def _():
                pltpu.make_async_copy(came[2 * t + side], target, sems.at[side]).start()

    for side, target in enumerate((right, left)):
        pltpu.make_async_copy(own.at[0], target, sems.at[side]).wait()


def endless_place_kernel(hold, count, meta, _, came_ref, out_ref, scratch, sem):
    chunk = scratch.shape[0]
    for s in range(CAP):
        for side in range(2):
            kind = meta[2 + s] - FAR * side
            for j in range(CHUNKS):
                t = kind - hold + j

                @pl.when((kind >= hold) & (kind < hold + FAR) & (t >= count))
                def _():
                    for copy in (
                        pltpu.make_async_copy(came_ref.at[side, t - count], scratch, sem),
                        pltpu.make_async_copy(scratch, out_ref.at[s, pl.ds(j * chunk, chunk)], sem),
                    ):
                        copy.start()
                        copy.wait()


def endless(meta, snd, update, came, out, n):
    hold, rows, cols = update.shape
    chunks = update.reshape(-1, rows // CHUNKS, cols)
    chunk = jax.ShapeDtypeStruct(chunks.shape[1:], update.dtype)
    arrived = [x for pair in came for x in pair]
    last = meta[2 + CAP + 2 * hold]

    def step(carry):
        t, kept = carry
        right, left = pl.pallas_call(
            functools.partial(endless_pick_kernel, len(came)),
            out_shape=[chunk, chunk],
            in_specs=[SMEM, SMEM] + [ANY] * (2 + len(arrived)),
            out_specs=[VMEM, VMEM],
            scratch_shapes=[pltpu.SemaphoreType.DMA((2,))],
            name="endless_pick",
        )(snd, t.reshape(1), chunks, kept, *arrived)
        both = jnp.stack(hop(right, left, n))[:, None]
        return t + 1, lax.dynamic_update_slice(kept, both, (0, t - STEPS, 0, 0))

    kept = jnp.zeros((2, snd.shape[1] - STEPS) + chunk.shape, update.dtype)
    _, kept = lax.while_loop(lambda carry: carry[0] < last, step, (jnp.int32(STEPS), kept))
    return pl.pallas_call(
        functools.partial(endless_place_kernel, hold, len(came)),
        out_shape=jax.ShapeDtypeStruct(out.shape, out.dtype),
        in_specs=[SMEM, ANY, ANY],
        out_specs=ANY,
        scratch_shapes=[pltpu.VMEM(chunk.shape, chunk.dtype), pltpu.SemaphoreType.DMA],
        input_output_aliases={1: 0},
        name="endless_place",
    )(meta, out, kept)[None]


def per_device(momentum, assignment):
    n = lax.axis_size("group")
    width = lax.axis_size("width")
    hold, rows, cols = momentum.shape
    where = jnp.stack([lax.axis_index("group"), lax.axis_index("width")]).astype(jnp.int32)
    snd, meta = make_plan(assignment, where, n, hold)
    keep, send, keeps, sends = partial_gram(meta, momentum, width)
    update, *done = one_update(meta, all_gather(reduce_scatter(keep, send, width), width), momentum, 0)
    pieces = all_gather(reduce_scatter(keeps, sends, width), width)
    for place_in_order in range(1, hold):
        (update,) = one_update(meta, pieces, momentum, place_in_order, update)
    chunks = update.reshape(-1, rows // CHUNKS, cols)
    came = []
    for step in range(STEPS):
        sent = (done[step], done[step]) if step < DELAY else pick(chunks, snd, came, step)
        came.append(hop(*sent, n))
    out = place(meta, came[:-1], update)
    out = place_last(meta, out, came[-1], STEPS - 1, hold)
    ways = [functools.partial(lambda extra, *args: stream(*args, extra, n), extra) for extra in EXTRA]
    ways.append(lambda *args: endless(*args, n))
    return update, lax.switch(meta[0], ways, meta, snd, update, came, out)


def solution(mesh):
    return jax.shard_map(
        per_device,
        mesh=mesh,
        in_specs=(P("group", None, "width"), P()),
        out_specs=(P("group", None, "width"), P("group", None, None, "width")),
        check_vma=False,
    )
```

```python
import functools
import math

import jax
import jax.numpy as jnp
from jax import lax
from jax.experimental import pallas as pl
from jax.experimental.pallas import tpu as pltpu
from jax.sharding import PartitionSpec as P

D = 7168
CAP = 2
CHUNKS = 2
DELAY = 2
STEPS = 4
EXTRA = (0, 2, 4, 6)
BLOCK = 256
SCALE = math.sqrt(D)
VMEM_BYTES = 56 * 1024 * 1024
NEVER = 1 << 20
FAR = 1 << 10
WORK = 5 * 10**9

SMEM = pl.BlockSpec(memory_space=pltpu.SMEM)
VMEM = pl.BlockSpec(memory_space=pltpu.VMEM)
ANY = pl.BlockSpec(memory_space=pl.ANY)


def compiler_params():
    return pltpu.CompilerParams(vmem_limit_bytes=VMEM_BYTES)


def most_steps(n, hold):
    end = 0
    for link in range(n - 1):
        load = min(hold * (link + 1), CAP * (n - 1 - link))
        end = max(CHUNKS, end - CHUNKS + DELAY) + CHUNKS * load
    return max(end, STEPS + max(EXTRA))


def plan_kernel(n, hold, assign, where, snd, meta, slot, key, ready, start, front):
    experts = n * hold
    me = where[0]
    names = [assign[e] for e in range(experts)]
    for e in range(experts):
        count = jnp.int32(0)
        for e2 in range(e):
            count += (names[e2] == names[e]).astype(jnp.int32)
        slot[e] = count
    for s in range(CAP):
        meta[2 + s] = -1
    for e in range(experts):

        @pl.when((names[e] == me) & (e // hold == me) & (slot[e] < CAP))
        def _():
            meta[2 + slot[e]] = e % hold

    for h in range(hold):
        meta[2 + CAP + h] = (assign[me * hold + h] >= 0).astype(jnp.int32)

    def crossing(e, side, link):
        owner = e // hold
        frm = owner if side == 0 else n - 1 - owner
        if frm > link:
            return None
        to = names[e] if side == 0 else n - 1 - names[e]
        return (names[e] >= 0) & (link < to)

    busy = []
    for side in range(2):
        most = jnp.int32(0)
        for link in range(n - 1):
            load = jnp.int32(0)
            for e in range(experts):
                here = crossing(e, side, link)
                if here is not None:
                    load += here.astype(jnp.int32)
            most = jnp.maximum(most, load)
        busy.append(most)

    for owner in range(n):
        best, chosen = jnp.int32(-2), jnp.int32(0)
        for h in range(hold):
            name = names[owner * hold + h]
            value = jnp.where(
                name > owner, busy[0] * 64 + name - owner, jnp.where(name < owner, busy[1] * 64 + owner - name, 0)
            )
            value = jnp.where(name < 0, -1, value)
            best, chosen = jnp.where(value > best, value, best), jnp.where(value > best, h, chosen)
        front[owner] = chosen
    chosen = front[me]
    meta[2 + CAP + hold] = chosen
    for place in range(1, hold):
        meta[2 + CAP + hold + place] = jnp.where(chosen >= place, place - 1, place)

    longest = jnp.int32(0)
    for side in range(2):
        mine = me if side == 0 else n - 1 - me

        def clear(t, _):
            snd[side, t] = 0
            return 0

        lax.fori_loop(0, snd.shape[1], clear, 0)
        for link in range(n - 1):
            for e in range(experts):
                here = crossing(e, side, link)
                if here is None:
                    key[e] = NEVER
                    continue
                owner = e // hold
                frm = owner if side == 0 else n - 1 - owner
                to = names[e] if side == 0 else n - 1 - names[e]
                if frm == link:
                    at = jnp.where(front[owner] == e % hold, 0, CHUNKS)
                else:
                    at = start[e] + DELAY
                ready[e] = at
                key[e] = jnp.where(here, at * 64 + (n - to), NEVER)

            def choose(_, cursor):
                low, e = key[0], jnp.int32(0)
                for e2 in range(1, experts):
                    better = key[e2] < low
                    low, e = jnp.where(better, key[e2], low), jnp.where(better, e2, e)
                begin = jnp.maximum(cursor, ready[e])

                @pl.when(low < NEVER)
                def _():
                    before = start[e]
                    key[e] = NEVER
                    start[e] = begin
                    local = e // hold == me
                    to = assign[e] if side == 0 else n - 1 - assign[e]

                    @pl.when(mine == link)
                    def _():
                        base = jnp.where(local, e % hold * CHUNKS, NEVER + before)
                        for j in range(CHUNKS):
                            snd[side, begin + j] = base + j

                    @pl.when((mine == link + 1) & (to == link + 1) & (slot[e] < CAP))
                    def _():
                        meta[2 + slot[e]] = hold + FAR * side + begin

                return jnp.where(low < NEVER, begin + CHUNKS, cursor)

            most = min(hold * (link + 1), CAP * (n - 1 - link))
            longest = jnp.maximum(longest, lax.fori_loop(0, most, choose, jnp.int32(0)))
    branch = jnp.int32(0)
    for extra in EXTRA:
        branch += (longest > STEPS + extra).astype(jnp.int32)
    meta[0] = branch
    meta[1] = where[1]
    meta[2 + CAP + 2 * hold] = longest


def make_plan(assignment, where, n, hold):
    i32 = jnp.int32
    return pl.pallas_call(
        functools.partial(plan_kernel, n, hold),
        out_shape=[
            jax.ShapeDtypeStruct((2, most_steps(n, hold)), i32),
            jax.ShapeDtypeStruct((3 + CAP + 2 * hold,), i32),
        ],
        in_specs=[SMEM, SMEM],
        out_specs=[SMEM] * 2,
        scratch_shapes=[pltpu.SMEM((n * hold,), i32) for _ in range(4)] + [pltpu.SMEM((n,), i32)],
        name="plan",
    )(assignment, where)


def pick_kernel(step, count, snd, own, *rest):
    came, (right, left, sems) = rest[: 2 * count], rest[-3:]
    for side, target in enumerate((right, left)):
        code = snd[side, step]

        @pl.when(code < NEVER)
        def _():
            pltpu.make_async_copy(own.at[code], target, sems.at[side]).start()

        for t in range(count):

            @pl.when(code == NEVER + t)
            def _():
                pltpu.make_async_copy(came[2 * t + side], target, sems.at[side]).start()

    for side, target in enumerate((right, left)):
        pltpu.make_async_copy(own.at[0], target, sems.at[side]).wait()


def pick(own, snd, came, step):
    count = max(step + 1 - DELAY, 0)
    earlier = [x for pair in came[:count] for x in pair]
    chunk = jax.ShapeDtypeStruct(own.shape[1:], own.dtype)
    return pl.pallas_call(
        functools.partial(pick_kernel, step, count),
        out_shape=[chunk, chunk],
        in_specs=[SMEM] + [ANY] * (1 + len(earlier)),
        out_specs=[VMEM, VMEM],
        scratch_shapes=[pltpu.SemaphoreType.DMA((2,))],
        cost_estimate=pl.CostEstimate(
            flops=0, bytes_accessed=1, transcendentals=0
        ),
        name="pick",
    )(snd, own, *earlier)


def hop(right, left, n):
    return (
        lax.ppermute(right, "group", [(i, i + 1) for i in range(n - 1)]),
        lax.ppermute(left, "group", [(i + 1, i) for i in range(n - 1)]),
    )


def place_kernel(hold, steps, meta, update_ref, *rest):
    came, (out_ref, sems) = rest[: 2 * steps], rest[-2:]
    chunk = out_ref.shape[1] // CHUNKS

    def target(s, j):
        return out_ref.at[s, pl.ds(j * chunk, chunk)]

    for s in range(CAP):
        kind = meta[2 + s]

        @pl.when((kind >= 0) & (kind < hold))
        def _():
            for j in range(CHUNKS):
                pltpu.make_async_copy(
                    update_ref.at[kind, pl.ds(j * chunk, chunk)], target(s, j), sems.at[s, j]
                ).start()

        for side in range(2):
            for j in range(CHUNKS):
                for t in range(j, steps):

                    @pl.when(kind == hold + FAR * side + t - j)
                    def _():
                        pltpu.make_async_copy(came[2 * t + side], target(s, j), sems.at[s, j]).start()

        @pl.when(kind < 0)
        def _():
            out_ref[s] = jnp.zeros(out_ref.shape[1:], out_ref.dtype)

    for s in range(CAP):
        kind = meta[2 + s]
        at = kind - hold
        at = jnp.where(at >= FAR, at - FAR, at)
        for j in range(CHUNKS):

            @pl.when((kind >= 0) & (at + j < steps))
            def _():
                pltpu.make_async_copy(came[0], target(s, j), sems.at[s, j]).wait()


def last_kernel(hold, last, meta, _, *rest):
    came, (out_ref, sems) = rest[:2], rest[2:]
    chunk = came[0].shape[0]
    for wait in (False, True):
        for s in range(CAP):
            for side in range(2):
                for j in range(CHUNKS):

                    @pl.when((meta[2 + s] >= hold) & (meta[2 + s] == hold + FAR * side + last - j))
                    def _():
                        copy = pltpu.make_async_copy(
                            came[side], out_ref.at[s, pl.ds(j * chunk, chunk)], sems.at[s]
                        )
                        copy.wait() if wait else copy.start()


def place(meta, came, update, after):
    hold, rows, cols = update.shape
    arrived = [x for pair in came for x in pair]
    return pl.pallas_call(
        functools.partial(place_kernel, hold, len(came)),
        out_shape=jax.ShapeDtypeStruct((CAP, rows, cols), update.dtype),
        in_specs=[SMEM, ANY] + [ANY] * (1 + len(arrived)),
        out_specs=VMEM,
        scratch_shapes=[pltpu.SemaphoreType.DMA((CAP, CHUNKS))],
        compiler_params=compiler_params(),
        cost_estimate=pl.CostEstimate(flops=WORK, bytes_accessed=1, transcendentals=0),
        name="place",
    )(meta, update, *arrived, after)


def place_last(meta, out, came, step, hold):
    return pl.pallas_call(
        functools.partial(last_kernel, hold, step),
        out_shape=jax.ShapeDtypeStruct(out.shape, out.dtype),
        in_specs=[SMEM, ANY, VMEM, VMEM],
        out_specs=ANY,
        scratch_shapes=[pltpu.SemaphoreType.DMA((CAP,))],
        input_output_aliases={1: 0},
        cost_estimate=pl.CostEstimate(flops=WORK, bytes_accessed=1, transcendentals=0),
        name="last",
    )(meta, out, *came)


def pieces_of(me, q, width):
    chips = width // 2
    core, chip = q // chips, q % chips
    return ((me & 1) ^ core) * chips + ((me >> 1) ^ chip)


def gram_kernel(blocks, width, meta, x_ref, *rest):
    outs, scratch = rest[:4], rest[4]
    high = BLOCK // width
    me = meta[1]
    rows = blocks * BLOCK
    for i in range(blocks):
        scratch[i, :, pl.ds(i * BLOCK, rows - i * BLOCK)] = lax.dot_general(
            x_ref[0, pl.ds(i * BLOCK, BLOCK), :],
            x_ref[0, pl.ds(i * BLOCK, rows - i * BLOCK), :],
            (((1,), (1,)), ((), ())),
            preferred_element_type=jnp.float32,
        ).astype(jnp.bfloat16)

    def sort(keep, send):
        for q in range(width):
            piece = pieces_of(me, q, width)
            out = keep if q < width // 2 else send
            base = q % (width // 2) * (blocks * (blocks + 1) // 2)
            for j in range(blocks):
                for i in range(j + 1):
                    at = base + j * (j + 1) // 2 + i
                    out[0, pl.ds(at * high, high), :] = scratch[
                        i, pl.ds(pl.multiple_of(piece * high, high), high), pl.ds(j * BLOCK, BLOCK)
                    ]

    pl.when(pl.program_id(0) == 0)(lambda: sort(*outs[:2]))
    pl.when(pl.program_id(0) > 0)(lambda: sort(*outs[2:]))


def partial_gram(meta, momentum, width):
    hold, rows, cols = momentum.shape
    blocks = rows // BLOCK
    packed = blocks * (blocks + 1) // 2 * BLOCK
    shapes = [jax.ShapeDtypeStruct((count, packed // 2, BLOCK), jnp.bfloat16) for count in (1, 1, hold - 1, hold - 1)]
    one = pl.BlockSpec((1, packed // 2, BLOCK), lambda e, meta: (0, 0, 0))
    others = pl.BlockSpec((1, packed // 2, BLOCK), lambda e, meta: (jnp.maximum(e - 1, 0), 0, 0))
    return pl.pallas_call(
        functools.partial(gram_kernel, blocks, width),
        grid_spec=pltpu.PrefetchScalarGridSpec(
            num_scalar_prefetch=1,
            grid=(hold,),
            in_specs=[pl.BlockSpec((1, rows, cols), lambda e, meta: (meta[2 + CAP + hold + e], 0, 0))],
            out_specs=[one, one, others, others],
            scratch_shapes=[pltpu.VMEM((blocks, BLOCK, rows), jnp.bfloat16)],
        ),
        out_shape=shapes,
        compiler_params=compiler_params(),
        cost_estimate=pl.CostEstimate(
            flops=2 * hold * packed * BLOCK * cols,
            bytes_accessed=2 * hold * (rows * cols + packed * BLOCK),
            transcendentals=0,
        ),
        name="gram",
    )(meta, momentum)


def exchange(x, other, width):
    return lax.ppermute(x, "width", [(i, i ^ other) for i in range(width)])


def reduce_scatter(keep, send, width):
    chips = width // 2
    high = keep.shape[1] // chips
    total = keep.astype(jnp.float32) + exchange(send, 1, width).astype(jnp.float32)
    mine = total[:, :high]
    for r in range(1, chips):
        piece = total[:, r * high : (r + 1) * high].astype(jnp.bfloat16)
        mine = mine + exchange(piece, 2 * r, width).astype(jnp.float32)
    return mine.astype(jnp.bfloat16)


def share_kernel(chips, keep, other, _, mine, *pieces):
    high = mine.shape[1]
    for r in range(chips):
        rows = pl.ds(r * high, high)
        total = keep[:, rows, :].astype(jnp.float32) + other[:, rows, :].astype(jnp.float32)
        if r == 0:
            mine[...] = total
        else:
            pieces[r - 1][...] = total.astype(jnp.bfloat16)


def total_kernel(mine, *rest):
    came, out = rest[:-2], rest[-1]
    total = mine[...]
    for other in came:
        total = total + other[...].astype(jnp.float32)
    out[...] = total.astype(jnp.bfloat16)


def reduce_scatter_late(keep, send, width, after_share, after_total):
    chips = width // 2
    shape = (keep.shape[0], keep.shape[1] // chips, keep.shape[2])
    half = jax.ShapeDtypeStruct(shape, jnp.bfloat16)
    mine, *pieces = pl.pallas_call(
        functools.partial(share_kernel, chips),
        out_shape=[jax.ShapeDtypeStruct(shape, jnp.float32)] + [half] * (chips - 1),
        in_specs=[VMEM, VMEM, ANY],
        out_specs=[VMEM] * chips,
        compiler_params=compiler_params(),
        name="share",
    )(keep, exchange(send, 1, width), after_share)
    came = [exchange(piece, 2 * r, width) for r, piece in enumerate(pieces, 1)]
    return pl.pallas_call(
        total_kernel,
        out_shape=half,
        in_specs=[VMEM] * chips + [ANY],
        out_specs=VMEM,
        compiler_params=compiler_params(),
        cost_estimate=pl.CostEstimate(flops=0, bytes_accessed=1, transcendentals=0),
        name="total",
    )(mine, *came, after_total)


def all_gather(x, width):
    pieces = [x] + [exchange(x, 2 * r, width) for r in range(1, width // 2)]
    return pieces + [exchange(piece, 1, width) for piece in pieces]


def unpack(blocks, width, me, pieces, gram_ref):
    high = BLOCK // width
    for q in range(width):
        piece = pieces_of(me, q, width)
        for j in range(blocks):
            for i in range(j + 1):
                at = j * (j + 1) // 2 + i
                gram_ref[
                    pl.ds(pl.multiple_of(i * BLOCK + piece * high, high), high), pl.ds(j * BLOCK, BLOCK)
                ] = pieces[q][0, pl.ds(at * high, high), :]
    for j in range(blocks):
        for i in range(j):
            gram_ref[pl.ds(j * BLOCK, BLOCK), pl.ds(i * BLOCK, BLOCK)] = gram_ref[
                pl.ds(i * BLOCK, BLOCK), pl.ds(j * BLOCK, BLOCK)
            ].T


def update_kernel(blocks, width, hold, place, meta, x_ref, *rest):
    pieces, (gram_ref, first_ref, second_ref, sems) = rest[:width], rest[-4:]
    outs = rest[width + (place > 0) : -4]
    chosen = meta[2 + CAP + hold + place]
    live = meta[2 + CAP + chosen]
    rows = x_ref.shape[1]
    chunk = rows // CHUNKS

    def copies(j):
        span = pl.ds(j * chunk, chunk)
        targets = [outs[0].at[chosen, span]]
        if place == 0:
            targets.append(outs[1 + j])
        return [pltpu.make_async_copy(second_ref.at[span], to, sems.at[j, i]) for i, to in enumerate(targets)]

    @pl.when(live == 1)
    def _():
        unpack(blocks, width, meta[1], pieces, gram_ref)
        for at in range(0, rows, BLOCK):
            span = pl.ds(at, BLOCK)
            first_ref[span, :] = jnp.dot(
                gram_ref[span, :], x_ref[0], preferred_element_type=jnp.float32
            ).astype(jnp.bfloat16)
        for j in range(CHUNKS):
            for at in range(j * chunk, (j + 1) * chunk, BLOCK):
                span = pl.ds(at, BLOCK)
                second = jnp.dot(gram_ref[span, :], first_ref[...], preferred_element_type=jnp.float32)
                x, first = x_ref[0, span, :].astype(jnp.float32), first_ref[span, :].astype(jnp.float32)
                mixed = 3.4445 * x - 4.775 * first + 2.0315 * second
                second_ref[span, :] = (SCALE * mixed).astype(jnp.bfloat16)
            for copy in copies(j):
                copy.start()

    @pl.when(live == 0)
    def _():
        second_ref[...] = jnp.zeros_like(second_ref)
        for j in range(CHUNKS):
            for copy in copies(j):
                copy.start()

    for j in range(CHUNKS):
        for copy in copies(j):
            copy.wait()


def one_update(meta, pieces, momentum, place, update=None):
    hold, rows, cols = momentum.shape
    index = max(place - 1, 0)
    width = len(pieces)
    out_shape = [jax.ShapeDtypeStruct(momentum.shape, momentum.dtype)]
    if place == 0:
        out_shape += [jax.ShapeDtypeStruct((rows // CHUNKS, cols), momentum.dtype)] * CHUNKS
    before = [] if update is None else [update]
    return pl.pallas_call(
        functools.partial(update_kernel, rows // BLOCK, width, hold, place),
        grid_spec=pltpu.PrefetchScalarGridSpec(
            num_scalar_prefetch=1,
            grid=(1,),
            in_specs=[pl.BlockSpec((1, rows, cols), lambda i, meta: (meta[2 + CAP + hold + place], 0, 0))]
            + [pl.BlockSpec((1,) + piece.shape[1:], lambda i, meta: (index, 0, 0)) for piece in pieces]
            + [ANY] * len(before),
            out_specs=[ANY] * len(out_shape),
            scratch_shapes=[
                pltpu.VMEM((rows, rows), jnp.bfloat16),
                pltpu.VMEM((rows, cols), jnp.bfloat16),
                pltpu.VMEM((rows, cols), jnp.bfloat16),
                pltpu.SemaphoreType.DMA((CHUNKS, 2)),
            ],
        ),
        out_shape=out_shape,
        input_output_aliases={2 + width: 0} if before else {},
        compiler_params=compiler_params(),
        cost_estimate=pl.CostEstimate(
            flops=0 if before else 4 * rows * rows * cols, bytes_accessed=1, transcendentals=0
        ),
        name="update",
    )(meta, momentum, *pieces, *before)


def stream(meta, snd, update, came, out, sent, extra, n):
    hold, rows, cols = update.shape
    chunks = update.reshape(-1, rows // CHUNKS, cols)
    came = list(came)
    for step in range(STEPS, STEPS + extra):
        came.append(hop(*(sent if step == STEPS else pick(chunks, snd, came, step)), n))
    for step in range(STEPS, STEPS + extra):
        out = place_last(meta, out, came[step], step, hold)
    return out[None]


def endless_pick_kernel(count, snd, step, own, came_in, *rest):
    came, (right, left, sems) = rest[:-3], rest[-3:]
    for side, target in enumerate((right, left)):
        code = snd[side, step[0]]

        @pl.when(code < NEVER)
        def _():
            pltpu.make_async_copy(own.at[code], target, sems.at[side]).start()

        @pl.when(code >= NEVER + count)
        def _():
            pltpu.make_async_copy(came_in.at[side, code - NEVER - count], target, sems.at[side]).start()

        for t in range(count):

            @pl.when(code == NEVER + t)
            def _():
                pltpu.make_async_copy(came[2 * t + side], target, sems.at[side]).start()

    for side, target in enumerate((right, left)):
        pltpu.make_async_copy(own.at[0], target, sems.at[side]).wait()


def endless_place_kernel(hold, count, meta, _, came_ref, out_ref, scratch, sem):
    chunk = scratch.shape[0]
    for s in range(CAP):
        for side in range(2):
            kind = meta[2 + s] - FAR * side
            for j in range(CHUNKS):
                t = kind - hold + j

                @pl.when((kind >= hold) & (kind < hold + FAR) & (t >= count))
                def _():
                    for copy in (
                        pltpu.make_async_copy(came_ref.at[side, t - count], scratch, sem),
                        pltpu.make_async_copy(scratch, out_ref.at[s, pl.ds(j * chunk, chunk)], sem),
                    ):
                        copy.start()
                        copy.wait()


def endless(meta, snd, update, came, out, _, n):
    hold, rows, cols = update.shape
    chunks = update.reshape(-1, rows // CHUNKS, cols)
    chunk = jax.ShapeDtypeStruct(chunks.shape[1:], update.dtype)
    arrived = [x for pair in came for x in pair]
    last = meta[2 + CAP + 2 * hold]

    def step(carry):
        t, kept = carry
        right, left = pl.pallas_call(
            functools.partial(endless_pick_kernel, len(came)),
            out_shape=[chunk, chunk],
            in_specs=[SMEM, SMEM] + [ANY] * (2 + len(arrived)),
            out_specs=[VMEM, VMEM],
            scratch_shapes=[pltpu.SemaphoreType.DMA((2,))],
            name="endless_pick",
        )(snd, t.reshape(1), chunks, kept, *arrived)
        both = jnp.stack(hop(right, left, n))[:, None]
        return t + 1, lax.dynamic_update_slice(kept, both, (0, t - STEPS, 0, 0))

    kept = jnp.zeros((2, snd.shape[1] - STEPS) + chunk.shape, update.dtype)
    _, kept = lax.while_loop(lambda carry: carry[0] < last, step, (jnp.int32(STEPS), kept))
    return pl.pallas_call(
        functools.partial(endless_place_kernel, hold, len(came)),
        out_shape=jax.ShapeDtypeStruct(out.shape, out.dtype),
        in_specs=[SMEM, ANY, ANY],
        out_specs=ANY,
        scratch_shapes=[pltpu.VMEM(chunk.shape, chunk.dtype), pltpu.SemaphoreType.DMA],
        input_output_aliases={1: 0},
        name="endless_place",
    )(meta, out, kept)[None]


def per_device(momentum, assignment):
    n = lax.axis_size("group")
    width = lax.axis_size("width")
    hold, rows, cols = momentum.shape
    where = jnp.stack([lax.axis_index("group"), lax.axis_index("width")]).astype(jnp.int32)
    snd, meta = make_plan(assignment, where, n, hold)
    keep, send, keeps, sends = partial_gram(meta, momentum, width)
    pieces = all_gather(reduce_scatter(keep, send, width), width)
    update, *done = one_update(meta, pieces, momentum, 0)
    pieces = all_gather(reduce_scatter_late(keeps, sends, width, pieces[1], done[0]), width)
    for place_in_order in range(1, hold):
        (update,) = one_update(meta, pieces, momentum, place_in_order, update)
    chunks = update.reshape(-1, rows // CHUNKS, cols)
    came = []
    for step in range(STEPS):
        sent = (done[step], done[step]) if step < DELAY else pick(chunks, snd, came, step)
        came.append(hop(*sent, n))
    sent = pick(chunks, snd, came, STEPS)
    out = place(meta, came[:-1], update, sent[0])
    out = place_last(meta, out, came[-1], STEPS - 1, hold)
    ways = [functools.partial(lambda extra, *args: stream(*args, extra, n), extra) for extra in EXTRA]
    ways.append(lambda *args: endless(*args, n))
    return update, lax.switch(meta[0], ways, meta, snd, update, came, out, sent)


def solution(mesh):
    return jax.shard_map(
        per_device,
        mesh=mesh,
        in_specs=(P("group", None, "width"), P()),
        out_specs=(P("group", None, "width"), P("group", None, None, "width")),
        check_vma=False,
    )
```

```python
import functools
import math

import jax
import jax.numpy as jnp
from jax import lax
from jax.experimental import pallas as pl
from jax.experimental.pallas import tpu as pltpu
from jax.sharding import PartitionSpec as P

D = 7168
CAP = 2
CHUNKS = 2
DELAY = 2
STEPS = 4
EXTRA = (0, 2, 4, 6)
BLOCK = 256
SCALE = math.sqrt(D)
VMEM_BYTES = 56 * 1024 * 1024
NEVER = 1 << 20
FAR = 1 << 10
WORK = 5 * 10**9

SMEM = pl.BlockSpec(memory_space=pltpu.SMEM)
VMEM = pl.BlockSpec(memory_space=pltpu.VMEM)
ANY = pl.BlockSpec(memory_space=pl.ANY)


def compiler_params():
    return pltpu.CompilerParams(vmem_limit_bytes=VMEM_BYTES)


def most_steps(n, hold):
    end = 0
    for link in range(n - 1):
        load = min(hold * (link + 1), CAP * (n - 1 - link))
        end = max(CHUNKS, end - CHUNKS + DELAY) + CHUNKS * load
    return max(end, STEPS + max(EXTRA))


def plan_kernel(n, hold, assign, where, snd, meta, slot, key, ready, start, front):
    experts = n * hold
    me = where[0]
    names = [assign[e] for e in range(experts)]
    for e in range(experts):
        count = jnp.int32(0)
        for e2 in range(e):
            count += (names[e2] == names[e]).astype(jnp.int32)
        slot[e] = count
    for s in range(CAP):
        meta[2 + s] = -1
    for e in range(experts):

        @pl.when((names[e] == me) & (e // hold == me) & (slot[e] < CAP))
        def _():
            meta[2 + slot[e]] = e % hold

    for h in range(hold):
        meta[2 + CAP + h] = (assign[me * hold + h] >= 0).astype(jnp.int32)

    def crossing(e, side, link):
        owner = e // hold
        frm = owner if side == 0 else n - 1 - owner
        if frm > link:
            return None
        to = names[e] if side == 0 else n - 1 - names[e]
        return (names[e] >= 0) & (link < to)

    busy = []
    for side in range(2):
        most = jnp.int32(0)
        for link in range(n - 1):
            load = jnp.int32(0)
            for e in range(experts):
                here = crossing(e, side, link)
                if here is not None:
                    load += here.astype(jnp.int32)
            most = jnp.maximum(most, load)
        busy.append(most)

    for owner in range(n):
        best, chosen = jnp.int32(-2), jnp.int32(0)
        for h in range(hold):
            name = names[owner * hold + h]
            value = jnp.where(
                name > owner, busy[0] * 64 + name - owner, jnp.where(name < owner, busy[1] * 64 + owner - name, 0)
            )
            value = jnp.where(name < 0, -1, value)
            best, chosen = jnp.where(value > best, value, best), jnp.where(value > best, h, chosen)
        front[owner] = chosen
    chosen = front[me]
    meta[2 + CAP + hold] = chosen
    for place in range(1, hold):
        meta[2 + CAP + hold + place] = jnp.where(chosen >= place, place - 1, place)

    longest = jnp.int32(0)
    for side in range(2):
        mine = me if side == 0 else n - 1 - me

        def clear(t, _):
            snd[side, t] = 0
            return 0

        lax.fori_loop(0, snd.shape[1], clear, 0)
        for link in range(n - 1):
            for e in range(experts):
                here = crossing(e, side, link)
                if here is None:
                    key[e] = NEVER
                    continue
                owner = e // hold
                frm = owner if side == 0 else n - 1 - owner
                to = names[e] if side == 0 else n - 1 - names[e]
                if frm == link:
                    at = jnp.where(front[owner] == e % hold, 0, CHUNKS)
                else:
                    at = start[e] + DELAY
                ready[e] = at
                key[e] = jnp.where(here, at * 64 + (n - to), NEVER)

            def choose(_, cursor):
                low, e = key[0], jnp.int32(0)
                for e2 in range(1, experts):
                    better = key[e2] < low
                    low, e = jnp.where(better, key[e2], low), jnp.where(better, e2, e)
                begin = jnp.maximum(cursor, ready[e])

                @pl.when(low < NEVER)
                def _():
                    before = start[e]
                    key[e] = NEVER
                    start[e] = begin
                    local = e // hold == me
                    to = assign[e] if side == 0 else n - 1 - assign[e]

                    @pl.when(mine == link)
                    def _():
                        base = jnp.where(local, e % hold * CHUNKS, NEVER + before)
                        for j in range(CHUNKS):
                            snd[side, begin + j] = base + j

                    @pl.when((mine == link + 1) & (to == link + 1) & (slot[e] < CAP))
                    def _():
                        meta[2 + slot[e]] = hold + FAR * side + begin

                return jnp.where(low < NEVER, begin + CHUNKS, cursor)

            most = min(hold * (link + 1), CAP * (n - 1 - link))
            longest = jnp.maximum(longest, lax.fori_loop(0, most, choose, jnp.int32(0)))
    branch = jnp.int32(0)
    for extra in EXTRA:
        branch += (longest > STEPS + extra).astype(jnp.int32)
    meta[0] = branch
    meta[1] = where[1]
    meta[2 + CAP + 2 * hold] = longest


def make_plan(assignment, where, n, hold):
    i32 = jnp.int32
    return pl.pallas_call(
        functools.partial(plan_kernel, n, hold),
        out_shape=[
            jax.ShapeDtypeStruct((2, most_steps(n, hold)), i32),
            jax.ShapeDtypeStruct((3 + CAP + 2 * hold,), i32),
        ],
        in_specs=[SMEM, SMEM],
        out_specs=[SMEM] * 2,
        scratch_shapes=[pltpu.SMEM((n * hold,), i32) for _ in range(4)] + [pltpu.SMEM((n,), i32)],
        name="plan",
    )(assignment, where)


def pick_kernel(step, count, snd, own, *rest):
    came, (right, left, sems) = rest[: 2 * count], rest[-3:]
    for side, target in enumerate((right, left)):
        code = snd[side, step]

        @pl.when(code < NEVER)
        def _():
            pltpu.make_async_copy(own.at[code], target, sems.at[side]).start()

        for t in range(count):

            @pl.when(code == NEVER + t)
            def _():
                pltpu.make_async_copy(came[2 * t + side], target, sems.at[side]).start()

    for side, target in enumerate((right, left)):
        pltpu.make_async_copy(own.at[0], target, sems.at[side]).wait()


def pick(own, snd, came, step):
    count = max(step + 1 - DELAY, 0)
    earlier = [x for pair in came[:count] for x in pair]
    chunk = jax.ShapeDtypeStruct(own.shape[1:], own.dtype)
    return pl.pallas_call(
        functools.partial(pick_kernel, step, count),
        out_shape=[chunk, chunk],
        in_specs=[SMEM] + [ANY] * (1 + len(earlier)),
        out_specs=[VMEM, VMEM],
        scratch_shapes=[pltpu.SemaphoreType.DMA((2,))],
        cost_estimate=pl.CostEstimate(
            flops=0, bytes_accessed=1, transcendentals=0
        ),
        name="pick",
    )(snd, own, *earlier)


def hop(right, left, n):
    return (
        lax.ppermute(right, "group", [(i, i + 1) for i in range(n - 1)]),
        lax.ppermute(left, "group", [(i + 1, i) for i in range(n - 1)]),
    )


def place_kernel(hold, steps, meta, update_ref, *rest):
    came, (out_ref, sems) = rest[: 2 * steps], rest[-2:]
    chunk = out_ref.shape[1] // CHUNKS

    def target(s, j):
        return out_ref.at[s, pl.ds(j * chunk, chunk)]

    for s in range(CAP):
        kind = meta[2 + s]

        @pl.when((kind >= 0) & (kind < hold))
        def _():
            for j in range(CHUNKS):
                pltpu.make_async_copy(
                    update_ref.at[kind, pl.ds(j * chunk, chunk)], target(s, j), sems.at[s, j]
                ).start()

        for side in range(2):
            for j in range(CHUNKS):
                for t in range(j, steps):

                    @pl.when(kind == hold + FAR * side + t - j)
                    def _():
                        pltpu.make_async_copy(came[2 * t + side], target(s, j), sems.at[s, j]).start()

        @pl.when(kind < 0)
        def _():
            out_ref[s] = jnp.zeros(out_ref.shape[1:], out_ref.dtype)

    for s in range(CAP):
        kind = meta[2 + s]
        at = kind - hold
        at = jnp.where(at >= FAR, at - FAR, at)
        for j in range(CHUNKS):

            @pl.when((kind >= 0) & (at + j < steps))
            def _():
                pltpu.make_async_copy(came[0], target(s, j), sems.at[s, j]).wait()


def last_kernel(hold, last, meta, _, *rest):
    came, (out_ref, sems) = rest[:2], rest[2:]
    chunk = came[0].shape[0]
    for wait in (False, True):
        for s in range(CAP):
            for side in range(2):
                for j in range(CHUNKS):

                    @pl.when((meta[2 + s] >= hold) & (meta[2 + s] == hold + FAR * side + last - j))
                    def _():
                        copy = pltpu.make_async_copy(
                            came[side], out_ref.at[s, pl.ds(j * chunk, chunk)], sems.at[s]
                        )
                        copy.wait() if wait else copy.start()


def place(meta, came, update, after):
    hold, rows, cols = update.shape
    arrived = [x for pair in came for x in pair]
    return pl.pallas_call(
        functools.partial(place_kernel, hold, len(came)),
        out_shape=jax.ShapeDtypeStruct((CAP, rows, cols), update.dtype),
        in_specs=[SMEM, ANY] + [ANY] * (1 + len(arrived)),
        out_specs=VMEM,
        scratch_shapes=[pltpu.SemaphoreType.DMA((CAP, CHUNKS))],
        compiler_params=compiler_params(),
        cost_estimate=pl.CostEstimate(flops=WORK, bytes_accessed=1, transcendentals=0),
        name="place",
    )(meta, update, *arrived, after)


def place_last(meta, out, came, step, hold):
    return pl.pallas_call(
        functools.partial(last_kernel, hold, step),
        out_shape=jax.ShapeDtypeStruct(out.shape, out.dtype),
        in_specs=[SMEM, ANY, VMEM, VMEM],
        out_specs=ANY,
        scratch_shapes=[pltpu.SemaphoreType.DMA((CAP,))],
        input_output_aliases={1: 0},
        cost_estimate=pl.CostEstimate(flops=WORK, bytes_accessed=1, transcendentals=0),
        name="last",
    )(meta, out, *came)


def pieces_of(me, q, width):
    chips = width // 2
    core, chip = q // chips, q % chips
    return ((me & 1) ^ core) * chips + ((me >> 1) ^ chip)


def gram_kernel(blocks, width, meta, x_ref, *rest):
    outs, scratch = rest[:4], rest[4]
    high = BLOCK // width
    me = meta[1]
    rows = blocks * BLOCK
    for i in range(blocks):
        scratch[i, :, pl.ds(i * BLOCK, rows - i * BLOCK)] = lax.dot_general(
            x_ref[0, pl.ds(i * BLOCK, BLOCK), :],
            x_ref[0, pl.ds(i * BLOCK, rows - i * BLOCK), :],
            (((1,), (1,)), ((), ())),
            preferred_element_type=jnp.float32,
        ).astype(jnp.bfloat16)

    def sort(keep, send):
        for q in range(width):
            piece = pieces_of(me, q, width)
            out = keep if q < width // 2 else send
            base = q % (width // 2) * (blocks * (blocks + 1) // 2)
            for j in range(blocks):
                for i in range(j + 1):
                    at = base + j * (j + 1) // 2 + i
                    out[0, pl.ds(at * high, high), :] = scratch[
                        i, pl.ds(pl.multiple_of(piece * high, high), high), pl.ds(j * BLOCK, BLOCK)
                    ]

    pl.when(pl.program_id(0) == 0)(lambda: sort(*outs[:2]))
    pl.when(pl.program_id(0) > 0)(lambda: sort(*outs[2:]))


def partial_gram(meta, momentum, width):
    hold, rows, cols = momentum.shape
    blocks = rows // BLOCK
    packed = blocks * (blocks + 1) // 2 * BLOCK
    shapes = [jax.ShapeDtypeStruct((count, packed // 2, BLOCK), jnp.bfloat16) for count in (1, 1, hold - 1, hold - 1)]
    one = pl.BlockSpec((1, packed // 2, BLOCK), lambda e, meta: (0, 0, 0))
    others = pl.BlockSpec((1, packed // 2, BLOCK), lambda e, meta: (jnp.maximum(e - 1, 0), 0, 0))
    return pl.pallas_call(
        functools.partial(gram_kernel, blocks, width),
        grid_spec=pltpu.PrefetchScalarGridSpec(
            num_scalar_prefetch=1,
            grid=(hold,),
            in_specs=[pl.BlockSpec((1, rows, cols), lambda e, meta: (meta[2 + CAP + hold + e], 0, 0))],
            out_specs=[one, one, others, others],
            scratch_shapes=[pltpu.VMEM((blocks, BLOCK, rows), jnp.bfloat16)],
        ),
        out_shape=shapes,
        compiler_params=compiler_params(),
        cost_estimate=pl.CostEstimate(
            flops=2 * hold * packed * BLOCK * cols,
            bytes_accessed=2 * hold * (rows * cols + packed * BLOCK),
            transcendentals=0,
        ),
        name="gram",
    )(meta, momentum)


def exchange(x, other, width):
    return lax.ppermute(x, "width", [(i, i ^ other) for i in range(width)])


def reduce_scatter(keep, send, width):
    chips = width // 2
    high = keep.shape[1] // chips
    total = keep.astype(jnp.float32) + exchange(send, 1, width).astype(jnp.float32)
    mine = total[:, :high]
    for r in range(1, chips):
        piece = total[:, r * high : (r + 1) * high].astype(jnp.bfloat16)
        mine = mine + exchange(piece, 2 * r, width).astype(jnp.float32)
    return mine.astype(jnp.bfloat16)


def share_kernel(chips, keep, other, _, mine, *pieces):
    high = mine.shape[1]
    for r in range(chips):
        rows = pl.ds(r * high, high)
        total = keep[:, rows, :].astype(jnp.float32) + other[:, rows, :].astype(jnp.float32)
        if r == 0:
            mine[...] = total
        else:
            pieces[r - 1][...] = total.astype(jnp.bfloat16)


def total_kernel(mine, *rest):
    came, out = rest[:-2], rest[-1]
    total = mine[...]
    for other in came:
        total = total + other[...].astype(jnp.float32)
    out[...] = total.astype(jnp.bfloat16)


def reduce_scatter_late(keep, send, width, after_share, after_total):
    chips = width // 2
    shape = (keep.shape[0], keep.shape[1] // chips, keep.shape[2])
    half = jax.ShapeDtypeStruct(shape, jnp.bfloat16)

    def block(shape):
        return pl.BlockSpec((1,) + shape[1:], lambda e: (e, 0, 0))

    mine, *pieces = pl.pallas_call(
        functools.partial(share_kernel, chips),
        grid=(shape[0],),
        out_shape=[jax.ShapeDtypeStruct(shape, jnp.float32)] + [half] * (chips - 1),
        in_specs=[block(keep.shape), block(keep.shape), ANY],
        out_specs=[block(shape)] * chips,
        compiler_params=compiler_params(),
        name="share",
    )(keep, exchange(send, 1, width), after_share)
    came = [exchange(piece, 2 * r, width) for r, piece in enumerate(pieces, 1)]
    return pl.pallas_call(
        total_kernel,
        grid=(shape[0],),
        out_shape=half,
        in_specs=[block(shape)] * chips + [ANY],
        out_specs=block(shape),
        compiler_params=compiler_params(),
        cost_estimate=pl.CostEstimate(flops=0, bytes_accessed=1, transcendentals=0),
        name="total",
    )(mine, *came, after_total)


def all_gather(x, width):
    pieces = [x] + [exchange(x, 2 * r, width) for r in range(1, width // 2)]
    return pieces + [exchange(piece, 1, width) for piece in pieces]


def unpack(blocks, width, me, pieces, gram_ref):
    high = BLOCK // width
    for q in range(width):
        piece = pieces_of(me, q, width)
        for j in range(blocks):
            for i in range(j + 1):
                at = j * (j + 1) // 2 + i
                gram_ref[
                    pl.ds(pl.multiple_of(i * BLOCK + piece * high, high), high), pl.ds(j * BLOCK, BLOCK)
                ] = pieces[q][0, pl.ds(at * high, high), :]
    for j in range(blocks):
        for i in range(j):
            gram_ref[pl.ds(j * BLOCK, BLOCK), pl.ds(i * BLOCK, BLOCK)] = gram_ref[
                pl.ds(i * BLOCK, BLOCK), pl.ds(j * BLOCK, BLOCK)
            ].T


def update_kernel(blocks, width, hold, place, meta, x_ref, *rest):
    pieces, (gram_ref, first_ref, second_ref, sems) = rest[:width], rest[-4:]
    outs = rest[width + (place > 0) : -4]
    chosen = meta[2 + CAP + hold + place]
    live = meta[2 + CAP + chosen]
    rows = x_ref.shape[1]
    chunk = rows // CHUNKS

    def copies(j):
        span = pl.ds(j * chunk, chunk)
        targets = [outs[0].at[chosen, span]]
        if place == 0:
            targets.append(outs[1 + j])
        return [pltpu.make_async_copy(second_ref.at[span], to, sems.at[j, i]) for i, to in enumerate(targets)]

    @pl.when(live == 1)
    def _():
        unpack(blocks, width, meta[1], pieces, gram_ref)
        for at in range(0, rows, BLOCK):
            span = pl.ds(at, BLOCK)
            first_ref[span, :] = jnp.dot(
                gram_ref[span, :], x_ref[0], preferred_element_type=jnp.float32
            ).astype(jnp.bfloat16)
        for j in range(CHUNKS):
            for at in range(j * chunk, (j + 1) * chunk, BLOCK):
                span = pl.ds(at, BLOCK)
                second = jnp.dot(gram_ref[span, :], first_ref[...], preferred_element_type=jnp.float32)
                x, first = x_ref[0, span, :].astype(jnp.float32), first_ref[span, :].astype(jnp.float32)
                mixed = 3.4445 * x - 4.775 * first + 2.0315 * second
                second_ref[span, :] = (SCALE * mixed).astype(jnp.bfloat16)
            for copy in copies(j):
                copy.start()

    @pl.when(live == 0)
    def _():
        second_ref[...] = jnp.zeros_like(second_ref)
        for j in range(CHUNKS):
            for copy in copies(j):
                copy.start()

    for j in range(CHUNKS):
        for copy in copies(j):
            copy.wait()


def one_update(meta, pieces, momentum, place, update=None):
    hold, rows, cols = momentum.shape
    index = max(place - 1, 0)
    width = len(pieces)
    out_shape = [jax.ShapeDtypeStruct(momentum.shape, momentum.dtype)]
    if place == 0:
        out_shape += [jax.ShapeDtypeStruct((rows // CHUNKS, cols), momentum.dtype)] * CHUNKS
    before = [] if update is None else [update]
    return pl.pallas_call(
        functools.partial(update_kernel, rows // BLOCK, width, hold, place),
        grid_spec=pltpu.PrefetchScalarGridSpec(
            num_scalar_prefetch=1,
            grid=(1,),
            in_specs=[pl.BlockSpec((1, rows, cols), lambda i, meta: (meta[2 + CAP + hold + place], 0, 0))]
            + [pl.BlockSpec((1,) + piece.shape[1:], lambda i, meta: (index, 0, 0)) for piece in pieces]
            + [ANY] * len(before),
            out_specs=[ANY] * len(out_shape),
            scratch_shapes=[
                pltpu.VMEM((rows, rows), jnp.bfloat16),
                pltpu.VMEM((rows, cols), jnp.bfloat16),
                pltpu.VMEM((rows, cols), jnp.bfloat16),
                pltpu.SemaphoreType.DMA((CHUNKS, 2)),
            ],
        ),
        out_shape=out_shape,
        input_output_aliases={2 + width: 0} if before else {},
        compiler_params=compiler_params(),
        cost_estimate=pl.CostEstimate(
            flops=0 if before else 4 * rows * rows * cols, bytes_accessed=1, transcendentals=0
        ),
        name="update",
    )(meta, momentum, *pieces, *before)


def rest_kernel(blocks, width, hold, meta, x_ref, *rest):
    pieces, (out_ref, gram_ref, first_ref) = rest[:width], rest[-3:]
    live = meta[2 + CAP + meta[2 + CAP + hold + 1 + pl.program_id(0)]]

    @pl.when(live == 1)
    def _():
        unpack(blocks, width, meta[1], pieces, gram_ref)
        for i in range(blocks):
            span = pl.ds(i * BLOCK, BLOCK)
            first_ref[span, :] = jnp.dot(
                gram_ref[span, :], x_ref[0], preferred_element_type=jnp.float32
            ).astype(jnp.bfloat16)
        for i in range(blocks):
            span = pl.ds(i * BLOCK, BLOCK)
            second = jnp.dot(gram_ref[span, :], first_ref[...], preferred_element_type=jnp.float32)
            x, first = x_ref[0, span, :].astype(jnp.float32), first_ref[span, :].astype(jnp.float32)
            mixed = 3.4445 * x - 4.775 * first + 2.0315 * second
            out_ref[0, span, :] = (SCALE * mixed).astype(jnp.bfloat16)

    @pl.when(live == 0)
    def _():
        out_ref[...] = jnp.zeros_like(out_ref)


def other_updates(meta, pieces, momentum, update):
    hold, rows, cols = momentum.shape
    width = len(pieces)
    block = pl.BlockSpec((1, rows, cols), lambda e, meta: (meta[2 + CAP + hold + 1 + e], 0, 0))
    return pl.pallas_call(
        functools.partial(rest_kernel, rows // BLOCK, width, hold),
        grid_spec=pltpu.PrefetchScalarGridSpec(
            num_scalar_prefetch=1,
            grid=(hold - 1,),
            in_specs=[block]
            + [pl.BlockSpec((1,) + piece.shape[1:], lambda e, meta: (e, 0, 0)) for piece in pieces]
            + [ANY],
            out_specs=block,
            scratch_shapes=[pltpu.VMEM((rows, rows), jnp.bfloat16), pltpu.VMEM((rows, cols), jnp.bfloat16)],
        ),
        out_shape=jax.ShapeDtypeStruct(update.shape, update.dtype),
        input_output_aliases={2 + width: 0},
        compiler_params=compiler_params(),
        cost_estimate=pl.CostEstimate(flops=0, bytes_accessed=1, transcendentals=0),
        name="others",
    )(meta, momentum, *pieces, update)


def stream(meta, snd, update, came, out, sent, extra, n):
    hold, rows, cols = update.shape
    chunks = update.reshape(-1, rows // CHUNKS, cols)
    came = list(came)
    for step in range(STEPS, STEPS + extra):
        came.append(hop(*(sent if step == STEPS else pick(chunks, snd, came, step)), n))
    for step in range(STEPS, STEPS + extra):
        out = place_last(meta, out, came[step], step, hold)
    return out[None]


def endless_pick_kernel(count, snd, step, own, came_in, *rest):
    came, (right, left, sems) = rest[:-3], rest[-3:]
    for side, target in enumerate((right, left)):
        code = snd[side, step[0]]

        @pl.when(code < NEVER)
        def _():
            pltpu.make_async_copy(own.at[code], target, sems.at[side]).start()

        @pl.when(code >= NEVER + count)
        def _():
            pltpu.make_async_copy(came_in.at[side, code - NEVER - count], target, sems.at[side]).start()

        for t in range(count):

            @pl.when(code == NEVER + t)
            def _():
                pltpu.make_async_copy(came[2 * t + side], target, sems.at[side]).start()

    for side, target in enumerate((right, left)):
        pltpu.make_async_copy(own.at[0], target, sems.at[side]).wait()


def endless_place_kernel(hold, count, meta, _, came_ref, out_ref, scratch, sem):
    chunk = scratch.shape[0]
    for s in range(CAP):
        for side in range(2):
            kind = meta[2 + s] - FAR * side
            for j in range(CHUNKS):
                t = kind - hold + j

                @pl.when((kind >= hold) & (kind < hold + FAR) & (t >= count))
                def _():
                    for copy in (
                        pltpu.make_async_copy(came_ref.at[side, t - count], scratch, sem),
                        pltpu.make_async_copy(scratch, out_ref.at[s, pl.ds(j * chunk, chunk)], sem),
                    ):
                        copy.start()
                        copy.wait()


def endless(meta, snd, update, came, out, _, n):
    hold, rows, cols = update.shape
    chunks = update.reshape(-1, rows // CHUNKS, cols)
    chunk = jax.ShapeDtypeStruct(chunks.shape[1:], update.dtype)
    arrived = [x for pair in came for x in pair]
    last = meta[2 + CAP + 2 * hold]

    def step(carry):
        t, kept = carry
        right, left = pl.pallas_call(
            functools.partial(endless_pick_kernel, len(came)),
            out_shape=[chunk, chunk],
            in_specs=[SMEM, SMEM] + [ANY] * (2 + len(arrived)),
            out_specs=[VMEM, VMEM],
            scratch_shapes=[pltpu.SemaphoreType.DMA((2,))],
            name="endless_pick",
        )(snd, t.reshape(1), chunks, kept, *arrived)
        both = jnp.stack(hop(right, left, n))[:, None]
        return t + 1, lax.dynamic_update_slice(kept, both, (0, t - STEPS, 0, 0))

    kept = jnp.zeros((2, snd.shape[1] - STEPS) + chunk.shape, update.dtype)
    _, kept = lax.while_loop(lambda carry: carry[0] < last, step, (jnp.int32(STEPS), kept))
    return pl.pallas_call(
        functools.partial(endless_place_kernel, hold, len(came)),
        out_shape=jax.ShapeDtypeStruct(out.shape, out.dtype),
        in_specs=[SMEM, ANY, ANY],
        out_specs=ANY,
        scratch_shapes=[pltpu.VMEM(chunk.shape, chunk.dtype), pltpu.SemaphoreType.DMA],
        input_output_aliases={1: 0},
        name="endless_place",
    )(meta, out, kept)[None]


def per_device(momentum, assignment):
    n = lax.axis_size("group")
    width = lax.axis_size("width")
    hold, rows, cols = momentum.shape
    where = jnp.stack([lax.axis_index("group"), lax.axis_index("width")]).astype(jnp.int32)
    snd, meta = make_plan(assignment, where, n, hold)
    keep, send, keeps, sends = partial_gram(meta, momentum, width)
    pieces = all_gather(reduce_scatter(keep, send, width), width)
    update, *done = one_update(meta, pieces, momentum, 0)
    pieces = all_gather(reduce_scatter_late(keeps, sends, width, pieces[width // 2 - 1], done[0]), width)
    update = other_updates(meta, pieces, momentum, update)
    chunks = update.reshape(-1, rows // CHUNKS, cols)
    came = []
    for step in range(STEPS):
        sent = (done[step], done[step]) if step < DELAY else pick(chunks, snd, came, step)
        came.append(hop(*sent, n))
    sent = pick(chunks, snd, came, STEPS)
    out = place(meta, came[:-1], update, sent[0])
    out = place_last(meta, out, came[-1], STEPS - 1, hold)
    ways = [functools.partial(lambda extra, *args: stream(*args, extra, n), extra) for extra in EXTRA]
    ways.append(lambda *args: endless(*args, n))
    return update, lax.switch(meta[0], ways, meta, snd, update, came, out, sent)


def solution(mesh):
    return jax.shard_map(
        per_device,
        mesh=mesh,
        in_specs=(P("group", None, "width"), P()),
        out_specs=(P("group", None, "width"), P("group", None, None, "width")),
        check_vma=False,
    )
```

```python
import functools
import math

import jax
import jax.numpy as jnp
from jax import lax
from jax.experimental import pallas as pl
from jax.experimental.pallas import tpu as pltpu
from jax.sharding import PartitionSpec as P

D = 7168
CAP = 2
CHUNKS = 2
DELAY = 2
STEPS = 4
EXTRA = (0, 2, 4, 6)
BLOCK = 256
SCALE = math.sqrt(D)
VMEM_BYTES = 56 * 1024 * 1024
NEVER = 1 << 20
FAR = 1 << 10
WORK = 5 * 10**9

SMEM = pl.BlockSpec(memory_space=pltpu.SMEM)
VMEM = pl.BlockSpec(memory_space=pltpu.VMEM)
ANY = pl.BlockSpec(memory_space=pl.ANY)


def compiler_params():
    return pltpu.CompilerParams(vmem_limit_bytes=VMEM_BYTES)


def most_steps(n, hold):
    end = 0
    for link in range(n - 1):
        load = min(hold * (link + 1), CAP * (n - 1 - link))
        end = max(CHUNKS, end - CHUNKS + DELAY) + CHUNKS * load
    return max(end, STEPS + max(EXTRA))


def plan_kernel(n, hold, assign, where, snd, meta, slot, key, ready, start, front):
    experts = n * hold
    me = where[0]
    names = [assign[e] for e in range(experts)]
    for e in range(experts):
        count = jnp.int32(0)
        for e2 in range(e):
            count += (names[e2] == names[e]).astype(jnp.int32)
        slot[e] = count
    for s in range(CAP):
        meta[2 + s] = -1
    for e in range(experts):

        @pl.when((names[e] == me) & (e // hold == me) & (slot[e] < CAP))
        def _():
            meta[2 + slot[e]] = e % hold

    for h in range(hold):
        meta[2 + CAP + h] = (assign[me * hold + h] >= 0).astype(jnp.int32)

    def crossing(e, side, link):
        owner = e // hold
        frm = owner if side == 0 else n - 1 - owner
        if frm > link:
            return None
        to = names[e] if side == 0 else n - 1 - names[e]
        return (names[e] >= 0) & (link < to)

    busy = []
    for side in range(2):
        most = jnp.int32(0)
        for link in range(n - 1):
            load = jnp.int32(0)
            for e in range(experts):
                here = crossing(e, side, link)
                if here is not None:
                    load += here.astype(jnp.int32)
            most = jnp.maximum(most, load)
        busy.append(most)

    for owner in range(n):
        best, chosen = jnp.int32(-2), jnp.int32(0)
        for h in range(hold):
            name = names[owner * hold + h]
            value = jnp.where(
                name > owner, busy[0] * 64 + name - owner, jnp.where(name < owner, busy[1] * 64 + owner - name, 0)
            )
            value = jnp.where(name < 0, -1, value)
            best, chosen = jnp.where(value > best, value, best), jnp.where(value > best, h, chosen)
        front[owner] = chosen
    chosen = front[me]
    meta[2 + CAP + hold] = chosen
    for place in range(1, hold):
        meta[2 + CAP + hold + place] = jnp.where(chosen >= place, place - 1, place)

    longest = jnp.int32(0)
    for side in range(2):
        mine = me if side == 0 else n - 1 - me

        def clear(t, _):
            snd[side, t] = 0
            return 0

        lax.fori_loop(0, snd.shape[1], clear, 0)
        for link in range(n - 1):
            for e in range(experts):
                here = crossing(e, side, link)
                if here is None:
                    key[e] = NEVER
                    continue
                owner = e // hold
                frm = owner if side == 0 else n - 1 - owner
                to = names[e] if side == 0 else n - 1 - names[e]
                if frm == link:
                    at = jnp.where(front[owner] == e % hold, 0, CHUNKS)
                else:
                    at = start[e] + DELAY
                ready[e] = at
                key[e] = jnp.where(here, at * 64 + (n - to), NEVER)

            def choose(_, cursor):
                low, e = key[0], jnp.int32(0)
                for e2 in range(1, experts):
                    better = key[e2] < low
                    low, e = jnp.where(better, key[e2], low), jnp.where(better, e2, e)
                begin = jnp.maximum(cursor, ready[e])

                @pl.when(low < NEVER)
                def _():
                    before = start[e]
                    key[e] = NEVER
                    start[e] = begin
                    local = e // hold == me
                    to = assign[e] if side == 0 else n - 1 - assign[e]

                    @pl.when(mine == link)
                    def _():
                        base = jnp.where(local, e % hold * CHUNKS, NEVER + before)
                        for j in range(CHUNKS):
                            snd[side, begin + j] = base + j

                    @pl.when((mine == link + 1) & (to == link + 1) & (slot[e] < CAP))
                    def _():
                        meta[2 + slot[e]] = hold + FAR * side + begin

                return jnp.where(low < NEVER, begin + CHUNKS, cursor)

            most = min(hold * (link + 1), CAP * (n - 1 - link))
            longest = jnp.maximum(longest, lax.fori_loop(0, most, choose, jnp.int32(0)))
    branch = jnp.int32(0)
    for extra in EXTRA:
        branch += (longest > STEPS + extra).astype(jnp.int32)
    meta[0] = branch
    meta[1] = where[1]
    meta[2 + CAP + 2 * hold] = longest


def make_plan(assignment, where, n, hold):
    i32 = jnp.int32
    return pl.pallas_call(
        functools.partial(plan_kernel, n, hold),
        out_shape=[
            jax.ShapeDtypeStruct((2, most_steps(n, hold)), i32),
            jax.ShapeDtypeStruct((3 + CAP + 2 * hold,), i32),
        ],
        in_specs=[SMEM, SMEM],
        out_specs=[SMEM] * 2,
        scratch_shapes=[pltpu.SMEM((n * hold,), i32) for _ in range(4)] + [pltpu.SMEM((n,), i32)],
        name="plan",
    )(assignment, where)


def pick_kernel(step, count, snd, own, *rest):
    came, (right, left, sems) = rest[: 2 * count], rest[-3:]
    for side, target in enumerate((right, left)):
        code = snd[side, step]

        @pl.when(code < NEVER)
        def _():
            pltpu.make_async_copy(own.at[code], target, sems.at[side]).start()

        for t in range(count):

            @pl.when(code == NEVER + t)
            def _():
                pltpu.make_async_copy(came[2 * t + side], target, sems.at[side]).start()

    for side, target in enumerate((right, left)):
        pltpu.make_async_copy(own.at[0], target, sems.at[side]).wait()


def pick(own, snd, came, step):
    count = max(step + 1 - DELAY, 0)
    earlier = [x for pair in came[:count] for x in pair]
    chunk = jax.ShapeDtypeStruct(own.shape[1:], own.dtype)
    return pl.pallas_call(
        functools.partial(pick_kernel, step, count),
        out_shape=[chunk, chunk],
        in_specs=[SMEM] + [ANY] * (1 + len(earlier)),
        out_specs=[VMEM, VMEM],
        scratch_shapes=[pltpu.SemaphoreType.DMA((2,))],
        cost_estimate=pl.CostEstimate(
            flops=0, bytes_accessed=1, transcendentals=0
        ),
        name="pick",
    )(snd, own, *earlier)


def hop(right, left, n):
    return (
        lax.ppermute(right, "group", [(i, i + 1) for i in range(n - 1)]),
        lax.ppermute(left, "group", [(i + 1, i) for i in range(n - 1)]),
    )


def place_kernel(hold, steps, meta, update_ref, *rest):
    came, (out_ref, sems) = rest[: 2 * steps], rest[-2:]
    chunk = out_ref.shape[1] // CHUNKS

    def target(s, j):
        return out_ref.at[s, pl.ds(j * chunk, chunk)]

    for s in range(CAP):
        kind = meta[2 + s]

        @pl.when((kind >= 0) & (kind < hold))
        def _():
            for j in range(CHUNKS):
                pltpu.make_async_copy(
                    update_ref.at[kind, pl.ds(j * chunk, chunk)], target(s, j), sems.at[s, j]
                ).start()

        for side in range(2):
            for j in range(CHUNKS):
                for t in range(j, steps):

                    @pl.when(kind == hold + FAR * side + t - j)
                    def _():
                        pltpu.make_async_copy(came[2 * t + side], target(s, j), sems.at[s, j]).start()

        @pl.when(kind < 0)
        def _():
            out_ref[s] = jnp.zeros(out_ref.shape[1:], out_ref.dtype)

    for s in range(CAP):
        kind = meta[2 + s]
        at = kind - hold
        at = jnp.where(at >= FAR, at - FAR, at)
        for j in range(CHUNKS):

            @pl.when((kind >= 0) & (at + j < steps))
            def _():
                pltpu.make_async_copy(came[0], target(s, j), sems.at[s, j]).wait()


def last_kernel(hold, last, meta, _, *rest):
    came, (out_ref, sems) = rest[:2], rest[2:]
    chunk = came[0].shape[0]
    for wait in (False, True):
        for s in range(CAP):
            for side in range(2):
                for j in range(CHUNKS):

                    @pl.when((meta[2 + s] >= hold) & (meta[2 + s] == hold + FAR * side + last - j))
                    def _():
                        copy = pltpu.make_async_copy(
                            came[side], out_ref.at[s, pl.ds(j * chunk, chunk)], sems.at[s]
                        )
                        copy.wait() if wait else copy.start()


def place(meta, came, update, after):
    hold, rows, cols = update.shape
    arrived = [x for pair in came for x in pair]
    return pl.pallas_call(
        functools.partial(place_kernel, hold, len(came)),
        out_shape=jax.ShapeDtypeStruct((CAP, rows, cols), update.dtype),
        in_specs=[SMEM, ANY] + [ANY] * (1 + len(arrived)),
        out_specs=VMEM,
        scratch_shapes=[pltpu.SemaphoreType.DMA((CAP, CHUNKS))],
        compiler_params=compiler_params(),
        cost_estimate=pl.CostEstimate(flops=WORK, bytes_accessed=1, transcendentals=0),
        name="place",
    )(meta, update, *arrived, after)


def place_last(meta, out, came, step, hold):
    return pl.pallas_call(
        functools.partial(last_kernel, hold, step),
        out_shape=jax.ShapeDtypeStruct(out.shape, out.dtype),
        in_specs=[SMEM, ANY, VMEM, VMEM],
        out_specs=ANY,
        scratch_shapes=[pltpu.SemaphoreType.DMA((CAP,))],
        input_output_aliases={1: 0},
        cost_estimate=pl.CostEstimate(flops=WORK, bytes_accessed=1, transcendentals=0),
        name="last",
    )(meta, out, *came)


def pieces_of(me, q, width):
    chips = width // 2
    core, chip = q // chips, q % chips
    return ((me & 1) ^ core) * chips + ((me >> 1) ^ chip)


def gram_kernel(blocks, width, meta, x_ref, *rest):
    outs, scratch = rest[:4], rest[4]
    high = BLOCK // width
    me = meta[1]
    rows = blocks * BLOCK
    for i in range(blocks):
        scratch[i, :, pl.ds(i * BLOCK, rows - i * BLOCK)] = lax.dot_general(
            x_ref[0, pl.ds(i * BLOCK, BLOCK), :],
            x_ref[0, pl.ds(i * BLOCK, rows - i * BLOCK), :],
            (((1,), (1,)), ((), ())),
            preferred_element_type=jnp.float32,
        ).astype(jnp.bfloat16)

    def sort(keep, send):
        for q in range(width):
            piece = pieces_of(me, q, width)
            out = keep if q < width // 2 else send
            base = q % (width // 2) * (blocks * (blocks + 1) // 2)
            for j in range(blocks):
                for i in range(j + 1):
                    at = base + j * (j + 1) // 2 + i
                    out[0, pl.ds(at * high, high), :] = scratch[
                        i, pl.ds(pl.multiple_of(piece * high, high), high), pl.ds(j * BLOCK, BLOCK)
                    ]

    pl.when(pl.program_id(0) == 0)(lambda: sort(*outs[:2]))
    pl.when(pl.program_id(0) > 0)(lambda: sort(*outs[2:]))


def partial_gram(meta, momentum, width):
    hold, rows, cols = momentum.shape
    blocks = rows // BLOCK
    packed = blocks * (blocks + 1) // 2 * BLOCK
    shapes = [jax.ShapeDtypeStruct((count, packed // 2, BLOCK), jnp.bfloat16) for count in (1, 1, hold - 1, hold - 1)]
    one = pl.BlockSpec((1, packed // 2, BLOCK), lambda e, meta: (0, 0, 0))
    others = pl.BlockSpec((1, packed // 2, BLOCK), lambda e, meta: (jnp.maximum(e - 1, 0), 0, 0))
    return pl.pallas_call(
        functools.partial(gram_kernel, blocks, width),
        grid_spec=pltpu.PrefetchScalarGridSpec(
            num_scalar_prefetch=1,
            grid=(hold,),
            in_specs=[pl.BlockSpec((1, rows, cols), lambda e, meta: (meta[2 + CAP + hold + e], 0, 0))],
            out_specs=[one, one, others, others],
            scratch_shapes=[pltpu.VMEM((blocks, BLOCK, rows), jnp.bfloat16)],
        ),
        out_shape=shapes,
        compiler_params=compiler_params(),
        cost_estimate=pl.CostEstimate(
            flops=2 * hold * packed * BLOCK * cols,
            bytes_accessed=2 * hold * (rows * cols + packed * BLOCK),
            transcendentals=0,
        ),
        name="gram",
    )(meta, momentum)


def exchange(x, other, width):
    return lax.ppermute(x, "width", [(i, i ^ other) for i in range(width)])


def reduce_scatter(keep, send, width):
    chips = width // 2
    high = keep.shape[1] // chips
    total = keep.astype(jnp.float32) + exchange(send, 1, width).astype(jnp.float32)
    mine = total[:, :high]
    for r in range(1, chips):
        piece = total[:, r * high : (r + 1) * high].astype(jnp.bfloat16)
        mine = mine + exchange(piece, 2 * r, width).astype(jnp.float32)
    return mine.astype(jnp.bfloat16)


def share_kernel(chips, keep, other, _, mine, *pieces):
    high = mine.shape[1]
    for r in range(chips):
        rows = pl.ds(r * high, high)
        total = keep[:, rows, :].astype(jnp.float32) + other[:, rows, :].astype(jnp.float32)
        if r == 0:
            mine[...] = total
        else:
            pieces[r - 1][...] = total.astype(jnp.bfloat16)


def total_kernel(mine, *rest):
    came, out = rest[:-2], rest[-1]
    total = mine[...]
    for other in came:
        total = total + other[...].astype(jnp.float32)
    out[...] = total.astype(jnp.bfloat16)


def reduce_scatter_late(keep, send, width, after_share, after_total):
    chips = width // 2
    shape = (keep.shape[0], keep.shape[1] // chips, keep.shape[2])
    half = jax.ShapeDtypeStruct(shape, jnp.bfloat16)

    def block(shape):
        return pl.BlockSpec((1,) + shape[1:], lambda e: (e, 0, 0))

    mine, *pieces = pl.pallas_call(
        functools.partial(share_kernel, chips),
        grid=(shape[0],),
        out_shape=[jax.ShapeDtypeStruct(shape, jnp.float32)] + [half] * (chips - 1),
        in_specs=[block(keep.shape), block(keep.shape), ANY],
        out_specs=[block(shape)] * chips,
        compiler_params=compiler_params(),
        name="share",
    )(keep, exchange(send, 1, width), after_share)
    came = [exchange(piece, 2 * r, width) for r, piece in enumerate(pieces, 1)]
    return pl.pallas_call(
        total_kernel,
        grid=(shape[0],),
        out_shape=half,
        in_specs=[block(shape)] * chips + [ANY],
        out_specs=block(shape),
        compiler_params=compiler_params(),
        cost_estimate=pl.CostEstimate(flops=0, bytes_accessed=1, transcendentals=0),
        name="total",
    )(mine, *came, after_total)


def all_gather(x, width):
    pieces = [x] + [exchange(x, 2 * r, width) for r in range(1, width // 2)]
    return pieces + [exchange(piece, 1, width) for piece in pieces]


def unpack(blocks, width, me, pieces, gram_ref):
    high = BLOCK // width
    for q in range(width):
        piece = pieces_of(me, q, width)
        for j in range(blocks):
            for i in range(j + 1):
                at = j * (j + 1) // 2 + i
                gram_ref[
                    pl.ds(pl.multiple_of(i * BLOCK + piece * high, high), high), pl.ds(j * BLOCK, BLOCK)
                ] = pieces[q][0, pl.ds(at * high, high), :]
    for j in range(blocks):
        for i in range(j):
            gram_ref[pl.ds(j * BLOCK, BLOCK), pl.ds(i * BLOCK, BLOCK)] = gram_ref[
                pl.ds(i * BLOCK, BLOCK), pl.ds(j * BLOCK, BLOCK)
            ].T


def update_kernel(blocks, width, hold, place, meta, x_ref, *rest):
    pieces, (gram_ref, first_ref, second_ref, sems) = rest[:width], rest[-4:]
    outs = rest[width + (place > 0) : -4]
    chosen = meta[2 + CAP + hold + place]
    live = meta[2 + CAP + chosen]
    rows = x_ref.shape[1]
    chunk = rows // CHUNKS

    def copies(at):
        span = pl.ds(at, BLOCK)
        targets = [outs[0].at[chosen, span]]
        if place == 0:
            targets.append(outs[1 + at // chunk].at[pl.ds(at % chunk, BLOCK)])
        return [
            pltpu.make_async_copy(second_ref.at[span], to, sems.at[at // BLOCK, i]) for i, to in enumerate(targets)
        ]

    @pl.when(live == 1)
    def _():
        unpack(blocks, width, meta[1], pieces, gram_ref)
        for at in range(0, rows, BLOCK):
            span = pl.ds(at, BLOCK)
            first_ref[span, :] = jnp.dot(
                gram_ref[span, :], x_ref[0], preferred_element_type=jnp.float32
            ).astype(jnp.bfloat16)
        for at in range(0, rows, BLOCK):
            span = pl.ds(at, BLOCK)
            second = jnp.dot(gram_ref[span, :], first_ref[...], preferred_element_type=jnp.float32)
            x, first = x_ref[0, span, :].astype(jnp.float32), first_ref[span, :].astype(jnp.float32)
            mixed = 3.4445 * x - 4.775 * first + 2.0315 * second
            second_ref[span, :] = (SCALE * mixed).astype(jnp.bfloat16)
            for copy in copies(at):
                copy.start()

    @pl.when(live == 0)
    def _():
        second_ref[...] = jnp.zeros_like(second_ref)
        for at in range(0, rows, BLOCK):
            for copy in copies(at):
                copy.start()

    for at in range(0, rows, BLOCK):
        for copy in copies(at):
            copy.wait()


def one_update(meta, pieces, momentum, place, update=None):
    hold, rows, cols = momentum.shape
    index = max(place - 1, 0)
    width = len(pieces)
    out_shape = [jax.ShapeDtypeStruct(momentum.shape, momentum.dtype)]
    if place == 0:
        out_shape += [jax.ShapeDtypeStruct((rows // CHUNKS, cols), momentum.dtype)] * CHUNKS
    before = [] if update is None else [update]
    return pl.pallas_call(
        functools.partial(update_kernel, rows // BLOCK, width, hold, place),
        grid_spec=pltpu.PrefetchScalarGridSpec(
            num_scalar_prefetch=1,
            grid=(1,),
            in_specs=[pl.BlockSpec((1, rows, cols), lambda i, meta: (meta[2 + CAP + hold + place], 0, 0))]
            + [pl.BlockSpec((1,) + piece.shape[1:], lambda i, meta: (index, 0, 0)) for piece in pieces]
            + [ANY] * len(before),
            out_specs=[ANY] * len(out_shape),
            scratch_shapes=[
                pltpu.VMEM((rows, rows), jnp.bfloat16),
                pltpu.VMEM((rows, cols), jnp.bfloat16),
                pltpu.VMEM((rows, cols), jnp.bfloat16),
                pltpu.SemaphoreType.DMA((rows // BLOCK, 2)),
            ],
        ),
        out_shape=out_shape,
        input_output_aliases={2 + width: 0} if before else {},
        compiler_params=compiler_params(),
        cost_estimate=pl.CostEstimate(
            flops=0 if before else 4 * rows * rows * cols, bytes_accessed=1, transcendentals=0
        ),
        name="update",
    )(meta, momentum, *pieces, *before)


def rest_kernel(blocks, width, hold, meta, x_ref, *rest):
    pieces, (out_ref, gram_ref, first_ref) = rest[:width], rest[-3:]
    live = meta[2 + CAP + meta[2 + CAP + hold + 1 + pl.program_id(0)]]

    @pl.when(live == 1)
    def _():
        unpack(blocks, width, meta[1], pieces, gram_ref)
        for i in range(blocks):
            span = pl.ds(i * BLOCK, BLOCK)
            first_ref[span, :] = jnp.dot(
                gram_ref[span, :], x_ref[0], preferred_element_type=jnp.float32
            ).astype(jnp.bfloat16)
        for i in range(blocks):
            span = pl.ds(i * BLOCK, BLOCK)
            second = jnp.dot(gram_ref[span, :], first_ref[...], preferred_element_type=jnp.float32)
            x, first = x_ref[0, span, :].astype(jnp.float32), first_ref[span, :].astype(jnp.float32)
            mixed = 3.4445 * x - 4.775 * first + 2.0315 * second
            out_ref[0, span, :] = (SCALE * mixed).astype(jnp.bfloat16)

    @pl.when(live == 0)
    def _():
        out_ref[...] = jnp.zeros_like(out_ref)


def other_updates(meta, pieces, momentum, update):
    hold, rows, cols = momentum.shape
    width = len(pieces)
    block = pl.BlockSpec((1, rows, cols), lambda e, meta: (meta[2 + CAP + hold + 1 + e], 0, 0))
    return pl.pallas_call(
        functools.partial(rest_kernel, rows // BLOCK, width, hold),
        grid_spec=pltpu.PrefetchScalarGridSpec(
            num_scalar_prefetch=1,
            grid=(hold - 1,),
            in_specs=[block]
            + [pl.BlockSpec((1,) + piece.shape[1:], lambda e, meta: (e, 0, 0)) for piece in pieces]
            + [ANY],
            out_specs=block,
            scratch_shapes=[pltpu.VMEM((rows, rows), jnp.bfloat16), pltpu.VMEM((rows, cols), jnp.bfloat16)],
        ),
        out_shape=jax.ShapeDtypeStruct(update.shape, update.dtype),
        input_output_aliases={2 + width: 0},
        compiler_params=compiler_params(),
        cost_estimate=pl.CostEstimate(flops=0, bytes_accessed=1, transcendentals=0),
        name="others",
    )(meta, momentum, *pieces, update)


def stream(meta, snd, update, came, out, sent, extra, n):
    hold, rows, cols = update.shape
    chunks = update.reshape(-1, rows // CHUNKS, cols)
    came = list(came)
    for step in range(STEPS, STEPS + extra):
        came.append(hop(*(sent if step == STEPS else pick(chunks, snd, came, step)), n))
    for step in range(STEPS, STEPS + extra):
        out = place_last(meta, out, came[step], step, hold)
    return out[None]


def endless_pick_kernel(count, snd, step, own, came_in, *rest):
    came, (right, left, sems) = rest[:-3], rest[-3:]
    for side, target in enumerate((right, left)):
        code = snd[side, step[0]]

        @pl.when(code < NEVER)
        def _():
            pltpu.make_async_copy(own.at[code], target, sems.at[side]).start()

        @pl.when(code >= NEVER + count)
        def _():
            pltpu.make_async_copy(came_in.at[side, code - NEVER - count], target, sems.at[side]).start()

        for t in range(count):

            @pl.when(code == NEVER + t)
            def _():
                pltpu.make_async_copy(came[2 * t + side], target, sems.at[side]).start()

    for side, target in enumerate((right, left)):
        pltpu.make_async_copy(own.at[0], target, sems.at[side]).wait()


def endless_place_kernel(hold, count, meta, _, came_ref, out_ref, scratch, sem):
    chunk = scratch.shape[0]
    for s in range(CAP):
        for side in range(2):
            kind = meta[2 + s] - FAR * side
            for j in range(CHUNKS):
                t = kind - hold + j

                @pl.when((kind >= hold) & (kind < hold + FAR) & (t >= count))
                def _():
                    for copy in (
                        pltpu.make_async_copy(came_ref.at[side, t - count], scratch, sem),
                        pltpu.make_async_copy(scratch, out_ref.at[s, pl.ds(j * chunk, chunk)], sem),
                    ):
                        copy.start()
                        copy.wait()


def endless(meta, snd, update, came, out, _, n):
    hold, rows, cols = update.shape
    chunks = update.reshape(-1, rows // CHUNKS, cols)
    chunk = jax.ShapeDtypeStruct(chunks.shape[1:], update.dtype)
    arrived = [x for pair in came for x in pair]
    last = meta[2 + CAP + 2 * hold]

    def step(carry):
        t, kept = carry
        right, left = pl.pallas_call(
            functools.partial(endless_pick_kernel, len(came)),
            out_shape=[chunk, chunk],
            in_specs=[SMEM, SMEM] + [ANY] * (2 + len(arrived)),
            out_specs=[VMEM, VMEM],
            scratch_shapes=[pltpu.SemaphoreType.DMA((2,))],
            name="endless_pick",
        )(snd, t.reshape(1), chunks, kept, *arrived)
        both = jnp.stack(hop(right, left, n))[:, None]
        return t + 1, lax.dynamic_update_slice(kept, both, (0, t - STEPS, 0, 0))

    kept = jnp.zeros((2, snd.shape[1] - STEPS) + chunk.shape, update.dtype)
    _, kept = lax.while_loop(lambda carry: carry[0] < last, step, (jnp.int32(STEPS), kept))
    return pl.pallas_call(
        functools.partial(endless_place_kernel, hold, len(came)),
        out_shape=jax.ShapeDtypeStruct(out.shape, out.dtype),
        in_specs=[SMEM, ANY, ANY],
        out_specs=ANY,
        scratch_shapes=[pltpu.VMEM(chunk.shape, chunk.dtype), pltpu.SemaphoreType.DMA],
        input_output_aliases={1: 0},
        name="endless_place",
    )(meta, out, kept)[None]


def per_device(momentum, assignment):
    n = lax.axis_size("group")
    width = lax.axis_size("width")
    hold, rows, cols = momentum.shape
    where = jnp.stack([lax.axis_index("group"), lax.axis_index("width")]).astype(jnp.int32)
    snd, meta = make_plan(assignment, where, n, hold)
    keep, send, keeps, sends = partial_gram(meta, momentum, width)
    pieces = all_gather(reduce_scatter(keep, send, width), width)
    update, *done = one_update(meta, pieces, momentum, 0)
    pieces = all_gather(reduce_scatter_late(keeps, sends, width, pieces[width // 2 - 1], done[0]), width)
    update = other_updates(meta, pieces, momentum, update)
    chunks = update.reshape(-1, rows // CHUNKS, cols)
    came = []
    for step in range(STEPS):
        sent = (done[step], done[step]) if step < DELAY else pick(chunks, snd, came, step)
        came.append(hop(*sent, n))
    sent = pick(chunks, snd, came, STEPS)
    out = place(meta, came[:-1], update, sent[0])
    out = place_last(meta, out, came[-1], STEPS - 1, hold)
    ways = [functools.partial(lambda extra, *args: stream(*args, extra, n), extra) for extra in EXTRA]
    ways.append(lambda *args: endless(*args, n))
    return update, lax.switch(meta[0], ways, meta, snd, update, came, out, sent)


def solution(mesh):
    return jax.shard_map(
        per_device,
        mesh=mesh,
        in_specs=(P("group", None, "width"), P()),
        out_specs=(P("group", None, "width"), P("group", None, None, "width")),
        check_vma=False,
    )
```
